32 devices in a mesh: grp: 1, row: 8 (over y, x, core), sub: 4 (over z).
Axes of the slice: x: 2, y: 2, z: 4, core: 2. Of those that a mesh axis runs over, the one named last changes fastest.
Arguments:
- pair: bfloat16 [128, 128, 128], P(('grp', 'row', 'sub')), may hold values from -6 to 6
- mask: int32 [128], P('grp'), may hold values from 0 to 1, as said below
- chain: int32 [128], P('grp'), may hold values from 0 to 3, never falling along the last dimension, each value on 1 to 64 neighbouring positions
- ln_gain: float32 [2, 128], replicated, may hold values from 0.5 to 1.5
- ln_shift: float32 [2, 128], replicated, may hold values from -2 to 2
- w_qkvg: bfloat16 [2, 128, 512], replicated, may hold values from -0.5 to 0.5
- gate_bias: float32 [2, 128], replicated, may hold values from -4 to 4
- w_bias: bfloat16 [2, 4, 128], replicated, may hold values from -1 to 1
- w_out: bfloat16 [2, 128, 128], replicated, may hold values from -0.5 to 0.5
- out_bias: float32 [2, 128], replicated, may hold values from -2 to 2
- chain_offset: float32 [2, 4], replicated, may hold values from -300 to 300
Outputs:
- pair_out: bfloat16 [128, 128, 128], P('grp', ('row', 'sub'))
The draws below stay inside these ranges and needn't reach their ends.
Inputs may be any that keep to these rules, and one draw needn't show every extreme that they name: mask[r] is 1 for r below some L with 64 <= L < 128, and 0 for the rest.
All inputs are finite; a program needn't handle non-finite values.
Results may differ from the reference program's by a relative error of at most 0.0061.
Values may be sent and summed in bfloat16 or wider, within the bound.
No kernel may reach another device: no remote copies, remote signals or barrier semaphores. Data moves between devices by JAX's collectives and lax.ppermute only.
A program may use at most 64 MiB of HBM per device.

```python
import math
import jax
import jax.numpy as jnp
import numpy as np
from jax import lax

C = 128
HEADS = 4
HEAD_DIM = 32
HD = 128
N = 128
CHAINS = 4


def draw_pair(key, part):
    values = jnp.clip(jax.random.normal(key, (N, N, C)), -6.0, 6.0)
    return values.astype(jnp.bfloat16)


def draw_mask(key, part):
    length = jax.random.randint(key, (), N // 2, N)
    return (jnp.arange(N) < length).astype(jnp.int32)


def draw_w_bias(key, part):
    values = jnp.clip(jax.random.normal(key, (2, HEADS, C)), -4.0, 4.0) * C ** (-0.5)
    return values.astype(jnp.bfloat16)


def draw_chain_offset(key, part):
    third_key = jax.random.fold_in(key, 2)
    values = jax.random.uniform(third_key, (2, HEADS), minval=-3.0, maxval=3.0)
    return values.astype(jnp.float32)


def profile(amount, total, reach, lean):
    loads = [(1 << 20) // math.isqrt(standing ** lean) + 1 for standing in range(2, amount + 1)]
    spare, holding = total - reach - (amount - 1), [1] * (amount - 1)
    while spare > 0:
        movable = [i for i in range(amount - 1) if holding[i] < reach]
        mass, left = sum([loads[i] for i in movable]), spare
        for i in movable:
            extra = min(reach - holding[i], max(1, left * loads[i] // mass), spare)
            holding[i] = holding[i] + extra
            spare = spare - extra
    return np.array([reach] + holding)


def uneven_parts(key, number_of, total, bound, lean):
    if number_of == 2:
        one = jax.random.randint(key, (), max(1, total - bound), min(bound, total - 1) + 1)
        return jnp.stack([one, total - one])
    sizes = jnp.asarray(profile(number_of, total, bound, lean), jnp.int32)
    pairs = (number_of - 1) // 2
    giver, taker = sizes[1:1 + 2 * pairs:2], sizes[2:2 + 2 * pairs:2]
    room = jnp.minimum(giver - 1, bound - taker)
    passed = jax.random.randint(jax.random.fold_in(key, 1), (pairs,), 0, 1 << 20) % (room + 1)
    sizes = sizes.at[1:1 + 2 * pairs:2].set(giver - passed).at[2:2 + 2 * pairs:2].set(taker + passed)
    return sizes[jax.random.permutation(jax.random.fold_in(key, 2), number_of)]


def centred(stream_key, shape, scale, most, dtype=jnp.bfloat16):
    result = jax.random.normal(stream_key, shape, jnp.float32) * scale
    return jnp.minimum(jnp.maximum(result, -most), most).astype(dtype)


def setup_inputs(seed: int = 0, part: int = 0) -> dict:
    key_of = jax.random.split(jax.random.key(seed), 12)
    part_keys = jax.random.split(jax.random.fold_in(key_of[11], part), 12)
    return {
        "pair": draw_pair(jax.random.fold_in(jax.random.fold_in(key_of[11], part), 71), part),
        "mask": draw_mask(jax.random.fold_in(jax.random.fold_in(key_of[11], part), 71), part),
        "chain": jnp.searchsorted(jnp.cumsum(uneven_parts(part_keys[2], CHAINS, N, N // 2, 0)), jnp.arange(N), side="right").astype(jnp.int32),
        "ln_gain": jnp.clip(1.0 + 0.1 * jax.random.normal(key_of[3], (2, C), jnp.float32), 0.5, 1.5),
        "ln_shift": centred(key_of[4], (2, C), 0.3, 2.0, jnp.float32),
        "w_qkvg": centred(key_of[5], (2, C, 4 * HD), C ** -0.5, 0.5),
        "gate_bias": centred(key_of[6], (2, HD), 1.0, 4.0, jnp.float32),
        "w_bias": draw_w_bias(jax.random.fold_in(key_of[11], 71), part),
        "w_out": centred(key_of[8], (2, HD, C), HD ** -0.5, 0.5),
        "out_bias": centred(key_of[9], (2, C), 0.3, 2.0, jnp.float32),
        "chain_offset": draw_chain_offset(jax.random.fold_in(key_of[11], 71), part),
    }


EPS = 1e-05

def layer_norm(entries, gain_row, shift_row):
    values = entries.astype(jnp.float32)
    middle = lax.optimization_barrier(jnp.mean(values, axis=-1, keepdims=True))
    spread = lax.optimization_barrier(jnp.mean(jnp.square(values - middle), axis=-1, keepdims=True))
    return ((values - middle) * lax.rsqrt(spread + EPS) * gain_row + shift_row).astype(jnp.bfloat16)

def softmax_weights(logits):
    maximum = lax.optimization_barrier(jnp.max(logits, axis=-1, keepdims=True))
    expon = jnp.exp(logits - maximum)
    return (expon / lax.optimization_barrier(jnp.sum(expon, axis=-1, keepdims=True))).astype(jnp.bfloat16)

def one_layer(pair_now, which_layer, mask, chain, ln_gain, ln_shift, w_qkvg, gate_bias, w_bias, w_out, out_bias, chain_offset):
    residues = pair_now.shape[0]
    block_rows = 4
    blocks = pair_now.reshape(residues // block_rows, block_rows, residues, C)
    gain_row = ln_gain[which_layer]
    shift_row = ln_shift[which_layer]

    def bias_block(row_block):
        normed = layer_norm(row_block, gain_row, shift_row)
        return jnp.einsum('hc,jkc->hjk', w_bias[which_layer].astype(jnp.float32), normed.astype(jnp.float32)).astype(jnp.bfloat16)
    bias_all = lax.map(bias_block, blocks)
    bias_all = jnp.transpose(bias_all, (1, 0, 2, 3)).reshape(HEADS, residues, residues)
    key_mask = jnp.where(mask > 0, 0.0, -1000000000.0).astype(jnp.float32)
    chain_cross = (chain[:, None] != chain[None, :]).astype(jnp.float32)
    column_scale = jnp.where(jnp.arange(4 * HD) < HD, HEAD_DIM ** (-0.5), 1.0).astype(jnp.float32)

    def attend(row_block):
        normed = layer_norm(row_block, gain_row, shift_row)
        projected = jnp.dot(normed.reshape(-1, C), w_qkvg[which_layer], preferred_element_type=jnp.float32)
        projected = (projected * column_scale).astype(jnp.bfloat16).reshape(block_rows, residues, 4 * HD)
        queries = projected[..., :HD].astype(jnp.float32).reshape(block_rows, residues, HEADS, HEAD_DIM)
        key_part = projected[..., HD:2 * HD].astype(jnp.float32).reshape(block_rows, residues, HEADS, HEAD_DIM)
        values = projected[..., 2 * HD:3 * HD].astype(jnp.float32).reshape(block_rows, residues, HEADS, HEAD_DIM)
        logits = jnp.einsum('ijhd,ikhd->ihjk', queries, key_part)
        logits = logits + bias_all.astype(jnp.float32)[None]
        logits = logits + chain_offset[which_layer][None, :, None, None] * chain_cross[None, None]
        logits = logits + key_mask
        weights = softmax_weights(logits)
        attended = jnp.einsum('ihjk,ikhd->ijhd', weights.astype(jnp.float32), values).reshape(block_rows, residues, HD)
        gate_part = jax.nn.sigmoid(projected[..., 3 * HD:].astype(jnp.float32) + gate_bias[which_layer])
        gated = (attended * gate_part).astype(jnp.bfloat16)
        update = jnp.dot(gated.reshape(-1, HD), w_out[which_layer], preferred_element_type=jnp.float32)
        update = update.reshape(block_rows, residues, C) + out_bias[which_layer]
        return (row_block.astype(jnp.float32) + update).astype(jnp.bfloat16)
    return lax.map(attend, blocks).reshape(residues, residues, C)

def reference(pair, mask, chain, ln_gain, ln_shift, w_qkvg, gate_bias, w_bias, w_out, out_bias, chain_offset):
    started = one_layer(pair, 0, mask, chain, ln_gain, ln_shift, w_qkvg, gate_bias, w_bias, w_out, out_bias, chain_offset)
    flipped = jnp.swapaxes(started, 0, 1)
    ended = one_layer(flipped, 1, mask, chain, ln_gain, ln_shift, w_qkvg, gate_bias, w_bias, w_out, out_bias, chain_offset)
    return jnp.swapaxes(ended, 0, 1)
```

```python
import functools

import jax
import jax.numpy as jnp
from jax import lax
from jax.experimental import pallas as pl
from jax.experimental.pallas import tpu as pltpu
from jax.sharding import PartitionSpec as P

C = 128
HEADS = 4
HEAD_DIM = 32
HD = 128
LANES = 128
EPS = 1e-05

F32 = jnp.float32
BF16 = jnp.bfloat16
NN = (((1,), (0,)), ((), ()))
NT = (((1,), (1,)), ((), ()))


def matmul(a, b, dims=NN):
    return lax.dot_general(a, b, dims, preferred_element_type=F32)


def layer_norm(values, gain_row, shift_row):
    middle = jnp.mean(values, axis=-1, keepdims=True)
    centred = values - middle
    spread = jnp.mean(jnp.square(centred), axis=-1, keepdims=True)
    return (centred * lax.rsqrt(spread + EPS) * gain_row + shift_row).astype(BF16)


def head_mask(head):
    lane = lax.broadcasted_iota(jnp.int32, (1, HD), 1)
    return jnp.where(lane // HEAD_DIM == head, 1.0, 0.0).astype(F32)


def each(count, unrolled, body):
    if unrolled:
        for index in range(count):
            body(index)
    else:
        lax.fori_loop(0, count, lambda index, _: (body(index), 0)[1], 0)


def column_of(row):
    n = row.shape[1]
    first = lax.broadcasted_iota(jnp.int32, (n, n), 0)
    second = lax.broadcasted_iota(jnp.int32, (n, n), 1)
    return jnp.sum(jnp.where(first == second, row, 0.0), axis=1, keepdims=True)


def fill_bias(layer, flip, received, wide, total, mask, chain, chain_offset):
    n = total.shape[1]
    parts, slots = received.shape[0], wide.shape[0] // received.shape[0]
    chain_row = chain[...].astype(F32)
    chain_column = column_of(chain_row)
    key_row = jnp.where(mask[...] > 0, 0.0, -1000000000.0).astype(F32)
    for tile in range(n // LANES):
        block = received[:, tile * slots : (tile + 1) * slots, :].astype(F32)
        wide[...] = block.reshape(parts * slots, LANES)
        span = slice(tile * LANES, (tile + 1) * LANES)
        cross = (chain_column[span] if flip else chain_column) != (
            chain_row if flip else chain_row[:, span]
        )
        for head in range(HEADS):
            known = jnp.where(cross, chain_offset[layer, head], 0.0)
            known = known + (key_row if flip else key_row[:, span])
            gathered = wide[pl.ds(head, n, stride=HEADS), :]
            if flip:
                first = head * n + tile * LANES
                total[first : first + LANES, :] = gathered.T + known
            else:
                total[head * n : (head + 1) * n, span] = gathered + known


def attend(normed, entries, layer, total, w_qkvg, gate_bias, w_out, out_bias):
    n = normed.shape[0]
    projected = matmul(normed, w_qkvg[layer])
    queries = projected[:, :HD] * (HEAD_DIM ** (-0.5))
    keys = projected[:, HD : 2 * HD].astype(BF16)
    values = projected[:, 2 * HD : 3 * HD]
    gates = projected[:, 3 * HD :].astype(BF16).astype(F32)
    attended = jnp.zeros((n, HD), F32)
    for head in range(HEADS):
        own = head_mask(head)
        logits = matmul((queries * own).astype(BF16), keys, NT)
        logits = logits + total[head * n : (head + 1) * n, :]
        expon = jnp.exp(logits - jnp.max(logits, axis=-1, keepdims=True))
        weights = (expon / jnp.sum(expon, axis=-1, keepdims=True)).astype(BF16)
        attended = attended + matmul(weights, (values * own).astype(BF16))
    gated = (attended * jax.nn.sigmoid(gates + gate_bias[layer : layer + 1, :])).astype(BF16)
    update = matmul(gated, w_out[layer]) + out_bias[layer : layer + 1, :]
    return (entries + update).astype(BF16)


def bias_rows(normed, w_bias, layer):
    return matmul(w_bias[layer], normed, NT)


def first_kernel(pair, ln_gain, ln_shift, w_bias, out, narrow):
    parts, n = out.shape[0], narrow.shape[1]
    rows, slots = pair.shape[0] // n, narrow.shape[0]
    for row in range(rows):
        entries = pair[row * n : (row + 1) * n, :].astype(F32)
        normed = layer_norm(entries, ln_gain[0:1, :], ln_shift[0:1, :])
        narrow[row * HEADS : (row + 1) * HEADS, :] = bias_rows(normed, w_bias, 0)
    for tile in range(n // LANES):
        block = narrow[:, tile * LANES : (tile + 1) * LANES].astype(BF16)
        out[:, tile * slots : (tile + 1) * slots, :] = jnp.broadcast_to(
            block[None], (parts, slots, LANES)
        )


def start_kernel(
    chain_offset, received, pair, mask, chain, ln_gain, ln_shift, w_qkvg, gate_bias, w_bias, w_out,
    out_bias, out, wide, total, narrow, column, packed, apart,
):
    parts, n = out.shape[0], total.shape[1]
    rows, slots = pair.shape[0] // n, narrow.shape[0]
    square = rows * rows
    fill_bias(0, False, received, wide, total, mask, chain, chain_offset)

    def row_step(row):
        here = pl.ds(pl.multiple_of(row * n, LANES), n)
        entries = pair[here, :].astype(F32)
        normed = layer_norm(entries, ln_gain[0:1, :], ln_shift[0:1, :])
        started = attend(normed, entries, 0, total, w_qkvg, gate_bias, w_out, out_bias).astype(F32)
        column[...] = started
        for place in range(rows):
            packed[pl.ds(row * rows + place, parts, stride=square), :] = column[
                pl.ds(place, parts, stride=rows), :
            ]
        normed = layer_norm(started, ln_gain[1:2, :], ln_shift[1:2, :])
        apart[row, :, :] = bias_rows(normed, w_bias, 1)

    each(rows, n <= LANES, row_step)
    for row in range(rows):
        narrow[row * HEADS : (row + 1) * HEADS, :] = apart[row, :, :]
    out[:, :square, :] = packed[...].reshape(parts, square, LANES).astype(BF16)
    for tile in range(n // LANES):
        block = narrow[:, tile * LANES : (tile + 1) * LANES].astype(BF16)
        first = square + tile * slots
        out[:, first : first + slots, :] = jnp.broadcast_to(block[None], (parts, slots, LANES))


def end_kernel(
    chain_offset, received, mask, chain, ln_gain, ln_shift, w_qkvg, gate_bias, w_out, out_bias, out,
    wide, total, packed, column,
):
    parts, n = received.shape[0], total.shape[1]
    rows = packed.shape[0] // n
    square = rows * rows
    fill_bias(
        1, True, received.at[:, square:, :], wide, total, mask, chain, chain_offset
    )
    packed[...] = received[:, :square, :].astype(F32).reshape(parts * square, LANES)

    def column_step(place):
        here = pl.ds(place, n, stride=rows)
        entries = packed[here, :]
        normed = layer_norm(entries, ln_gain[1:2, :], ln_shift[1:2, :])
        ended = attend(normed, entries, 1, total, w_qkvg, gate_bias, w_out, out_bias)
        packed[here, :] = ended.astype(F32)

    each(rows, n <= LANES, column_step)
    out[...] = packed[...].astype(BF16)


def call(kernel, out_shape, scratch, operands, scalars=1):
    specs = [pl.BlockSpec(memory_space=pltpu.SMEM)] * scalars
    specs += [pl.BlockSpec(memory_space=pltpu.VMEM)] * (len(operands) - scalars)
    return pl.pallas_call(
        kernel,
        out_shape=out_shape,
        in_specs=specs,
        out_specs=pl.BlockSpec(memory_space=pltpu.VMEM),
        scratch_shapes=scratch,
        compiler_params=pltpu.CompilerParams(vmem_limit_bytes=40 * 1024 * 1024),
    )(*operands)


def local(
    pair, mask, chain, ln_gain, ln_shift, w_qkvg, gate_bias, w_bias, w_out, out_bias, chain_offset
):
    rows, n = pair.shape[0], pair.shape[1]
    parts = lax.axis_size("row") * lax.axis_size("sub")
    tiles, slots, square = n // LANES, rows * HEADS, rows * rows
    exchange = functools.partial(
        lax.all_to_all, axis_name=("row", "sub"), split_axis=0, concat_axis=0, tiled=True
    )
    flat = pair.reshape(rows * n, C)
    mask_row, chain_row = mask.reshape(1, n), chain.reshape(1, n)
    shared = [
        pltpu.VMEM((parts * slots, LANES), F32),
        pltpu.VMEM((HEADS * n, n), F32),
    ]
    bias_part = call(
        first_kernel,
        jax.ShapeDtypeStruct((parts, tiles * slots, LANES), BF16),
        [pltpu.VMEM((slots, n), F32)],
        (flat, ln_gain, ln_shift, w_bias),
        scalars=0,
    )
    bias_all = exchange(bias_part)
    sent = call(
        start_kernel,
        jax.ShapeDtypeStruct((parts, square + tiles * slots, LANES), BF16),
        shared
        + [
            pltpu.VMEM((slots, n), F32),
            pltpu.VMEM((n, C), F32),
            pltpu.VMEM((rows * n, C), F32),
            pltpu.VMEM((rows, HEADS, n), F32),
        ],
        (
            chain_offset, bias_all, flat, mask_row, chain_row, ln_gain, ln_shift, w_qkvg, gate_bias,
            w_bias, w_out, out_bias,
        ),
    )
    columns = exchange(sent)
    ended = call(
        end_kernel,
        jax.ShapeDtypeStruct((n * rows, C), BF16),
        shared + [pltpu.VMEM((rows * n, C), F32), pltpu.VMEM((n, C), F32)],
        (
            chain_offset, columns, mask_row, chain_row, ln_gain, ln_shift, w_qkvg, gate_bias, w_out,
            out_bias,
        ),
    )
    return ended.reshape(n, rows, C)


def solution(mesh):
    in_specs = (
        P(("grp", "row", "sub"), None, None),
        P("grp"),
        P("grp"),
        P(),
        P(),
        P(),
        P(),
        P(),
        P(),
        P(),
        P(),
    )
    out_specs = P("grp", ("row", "sub"), None)
    return jax.shard_map(local, mesh=mesh, in_specs=in_specs, out_specs=out_specs, check_vma=False)
```

```python
import functools

import jax
import jax.numpy as jnp
from jax import lax
from jax.experimental import pallas as pl
from jax.experimental.pallas import tpu as pltpu
from jax.sharding import PartitionSpec as P

C = 128
HEADS = 4
HEAD_DIM = 32
HD = 128
LANES = 128
EPS = 1e-05

F32 = jnp.float32
BF16 = jnp.bfloat16
NN = (((1,), (0,)), ((), ()))
NT = (((1,), (1,)), ((), ()))


def matmul(a, b, dims=NN):
    return lax.dot_general(a, b, dims, preferred_element_type=F32)


def layer_norm(values, gain_row, shift_row):
    middle = jnp.mean(values, axis=-1, keepdims=True)
    centred = values - middle
    spread = jnp.mean(jnp.square(centred), axis=-1, keepdims=True)
    return (centred * lax.rsqrt(spread + EPS) * gain_row + shift_row).astype(BF16)


def head_mask(head):
    lane = lax.broadcasted_iota(jnp.int32, (1, HD), 1)
    return jnp.where(lane // HEAD_DIM == head, 1.0, 0.0).astype(F32)


def each(count, unrolled, body):
    if unrolled:
        for index in range(count):
            body(index)
    else:
        lax.fori_loop(0, count, lambda index, _: (body(index), 0)[1], 0)


def block(index, size):
    if isinstance(index, int):
        return slice(index * size, (index + 1) * size)
    return pl.ds(pl.multiple_of(index * size, size), size)


def column_of(row):
    n = row.shape[1]
    first = lax.broadcasted_iota(jnp.int32, (n, n), 0)
    second = lax.broadcasted_iota(jnp.int32, (n, n), 1)
    return jnp.sum(jnp.where(first == second, row, 0.0), axis=1, keepdims=True)


def known_logits(layer, mask, chain, chain_offset, total):
    n = total.shape[1]
    chain_row = chain[...].astype(F32)
    key_row = jnp.where(mask[...] > 0, 0.0, -1000000000.0).astype(F32)
    cross = column_of(chain_row) != chain_row
    for head in range(HEADS):
        total[block(head, n), :] = jnp.where(cross, chain_offset[layer, head], 0.0) + key_row


def add_bias(flip, received, first_slot, wide, known, total):
    n = total.shape[1]
    parts, slots = received.shape[0], wide.shape[0] // received.shape[0]
    for tile in range(n // LANES):
        first = first_slot + tile * slots
        wide[...] = received[:, first : first + slots, :].astype(F32).reshape(parts * slots, LANES)
        span = block(tile, LANES)
        for head in range(HEADS):
            gathered = wide[pl.ds(head, n, stride=HEADS), :]
            if flip:
                here = block(head * (n // LANES) + tile, LANES)
                total[here, :] = gathered.T + known[here, :]
            else:
                here = block(head, n)
                total[here, span] = gathered + known[here, span]


def project(normed, weights, gate_row, queries, keys, values, gates):
    n = normed.shape[0]
    projected = matmul(normed, weights)
    scaled = projected[:, :HD] * (HEAD_DIM ** (-0.5))
    keys[...] = projected[:, HD : 2 * HD].astype(BF16)
    held = projected[:, 2 * HD : 3 * HD]
    gates[...] = jax.nn.sigmoid(projected[:, 3 * HD :].astype(BF16).astype(F32) + gate_row)
    for head in range(HEADS):
        own = head_mask(head)
        queries[block(head, n), :] = (scaled * own).astype(BF16)
        values[block(head, n), :HD] = (held * own).astype(BF16)
        values[block(head, n), HD:] = jnp.broadcast_to(own.astype(BF16), (n, HD))


def attend(queries, keys, values, gates, total, w_out, out_row):
    n = keys.shape[0]
    logits = matmul(queries[...], keys[...], NT) + total[...]
    expon = jnp.exp(logits - jnp.max(logits, axis=-1, keepdims=True)).astype(BF16)
    beside = jnp.concatenate([expon[block(head, n), :] for head in range(HEADS)], axis=1)
    summed = matmul(beside, values[...])
    gated = (summed[:, :HD] / summed[:, HD:] * gates[...]).astype(BF16)
    return matmul(gated, w_out) + out_row


def bias_rows(normed, w_bias, layer):
    return matmul(w_bias[layer], normed, NT)


def pack_bias(narrow, first_slot, out):
    parts, (slots, n) = out.shape[0], narrow.shape
    for tile in range(n // LANES):
        part = narrow[:, block(tile, LANES)].astype(BF16)
        first = first_slot + tile * slots
        out[:, first : first + slots, :] = jnp.broadcast_to(part[None], (parts, slots, LANES))


def fetch(pairs, sems):
    copies = [
        pltpu.make_async_copy(far, near, sems.at[index]) for index, (far, near) in enumerate(pairs)
    ]
    for copy in copies:
        copy.start()
    return copies


def bias_kernel(
    pair_far, gain_far, shift_far, bias_far, out, normed_out, pair, ln_gain, ln_shift, w_bias, narrow, sems
):
    n = narrow.shape[1]
    far, near = (pair_far, gain_far, shift_far, bias_far), (pair, ln_gain, ln_shift, w_bias)
    for copy in fetch(zip(far, near, strict=True), sems):
        copy.wait()
    for row in range(pair.shape[0] // n):
        entries = pair[block(row, n), :].astype(F32)
        normed = layer_norm(entries, ln_gain[0:1, :], ln_shift[0:1, :])
        normed_out[block(row, n), :] = normed
        narrow[block(row, HEADS), :] = bias_rows(normed, w_bias, 0)
    pack_bias(narrow, 0, out)


def project_kernel(
    offset_far, mask_far, chain_far, w_far, gate_far, w_out_far, out_bias_far, normed,
    queries, keys, values, gates, known_start, known_end, w_qkvg, gate_bias, w_out, out_bias,
    chain_offset, mask, chain, sems,
):
    n = known_start.shape[1]
    far = (w_far, gate_far, offset_far, mask_far, chain_far, w_out_far, out_bias_far)
    near = (w_qkvg, gate_bias, chain_offset, mask, chain, w_out, out_bias)
    copies = fetch(zip(far, near, strict=True), sems)
    copies[0].wait()
    copies[1].wait()

    def row_step(row):
        here, wide = block(row, n), block(row, HEADS * n)
        project(
            normed[here, :], w_qkvg[0], gate_bias[0:1, :], queries.at[wide, :], keys.at[here, :],
            values.at[wide, :], gates.at[here, :],
        )

    each(keys.shape[0] // n, n <= LANES, row_step)
    for copy in copies[2:]:
        copy.wait()
    known_logits(0, mask, chain, chain_offset, known_start)
    known_logits(1, mask, chain, chain_offset, known_end)


def start_kernel(
    received, pair, queries, keys, values, gates, known, ln_gain, ln_shift, w_bias, w_out, out_bias,
    out, wide, total, narrow, column, packed, apart,
):
    parts, n = out.shape[0], total.shape[1]
    rows = pair.shape[0] // n
    square = rows * rows
    add_bias(False, received, 0, wide, known, total)

    def row_step(row):
        here, broad = block(row, n), block(row, HEADS * n)
        update = attend(
            queries.at[broad, :], keys.at[here, :], values.at[broad, :], gates.at[here, :], total,
            w_out[0], out_bias[0:1, :],
        )
        started = (pair[here, :].astype(F32) + update).astype(BF16).astype(F32)
        column[here, :] = started
        first = row * n
        for place in range(rows):
            packed[pl.ds(row * rows + place, parts, stride=square), :] = column[
                pl.ds(first + place, parts, stride=rows), :
            ]
        normed = layer_norm(started, ln_gain[1:2, :], ln_shift[1:2, :])
        apart[row, :, :] = bias_rows(normed, w_bias, 1)

    each(rows, n <= LANES, row_step)
    for row in range(rows):
        narrow[block(row, HEADS), :] = apart[row, :, :]
    out[:, :square, :] = packed[...].reshape(parts, square, LANES).astype(BF16)
    pack_bias(narrow, square, out)


def end_kernel(
    received, known, ln_gain, ln_shift, w_qkvg, gate_bias, w_out, out_bias, out, wide, total, packed,
    queries, keys, values, gates,
):
    parts, n = received.shape[0], total.shape[1]
    rows = packed.shape[0] // n
    square = rows * rows
    packed[...] = received[:, :square, :].astype(F32).reshape(parts * square, LANES)

    def project_step(place):
        here, broad = block(place, n), block(place, HEADS * n)
        entries = packed[pl.ds(place, n, stride=rows), :]
        normed = layer_norm(entries, ln_gain[1:2, :], ln_shift[1:2, :])
        project(
            normed, w_qkvg[1], gate_bias[1:2, :], queries.at[broad, :], keys.at[here, :],
            values.at[broad, :], gates.at[here, :],
        )

    each(rows, n <= LANES, project_step)
    add_bias(True, received, square, wide, known, total)

    def column_step(place):
        here, broad = block(place, n), block(place, HEADS * n)
        update = attend(
            queries.at[broad, :], keys.at[here, :], values.at[broad, :], gates.at[here, :], total,
            w_out[1], out_bias[1:2, :],
        )
        stripe = pl.ds(place, n, stride=rows)
        packed[stripe, :] = packed[stripe, :] + update

    each(rows, n <= LANES, column_step)
    out[...] = packed[...].astype(BF16)


NEAR = pl.BlockSpec(memory_space=pltpu.VMEM)
FAR = pl.BlockSpec(memory_space=pltpu.HBM)


def call(kernel, out_shape, scratch, far, near):
    far = [pltpu.with_memory_space_constraint(array, pltpu.HBM) for array in far]
    return pl.pallas_call(
        kernel,
        out_shape=out_shape,
        in_specs=[FAR] * len(far) + [NEAR] * len(near),
        out_specs=jax.tree.map(lambda _: NEAR, out_shape),
        scratch_shapes=scratch,
        compiler_params=pltpu.CompilerParams(vmem_limit_bytes=40 * 1024 * 1024),
    )(*far, *near)


def local(
    pair, mask, chain, ln_gain, ln_shift, w_qkvg, gate_bias, w_bias, w_out, out_bias, chain_offset
):
    rows, n = pair.shape[0], pair.shape[1]
    parts = lax.axis_size("row") * lax.axis_size("sub")
    tiles, slots, square = n // LANES, rows * HEADS, rows * rows
    exchange = functools.partial(
        lax.all_to_all, axis_name=("row", "sub"), split_axis=0, concat_axis=0, tiled=True
    )
    shape = jax.ShapeDtypeStruct

    def like(*arrays):
        return [shape(array.shape, array.dtype) for array in arrays]

    flat = pair.reshape(rows * n, C)
    mask_row, chain_row = mask.reshape(1, n), chain.reshape(1, n)
    wide = pltpu.VMEM((parts * slots, LANES), F32)
    total = pltpu.VMEM((HEADS * n, n), F32)
    narrow = pltpu.VMEM((slots, n), F32)
    entries = pltpu.VMEM((rows * n, C), F32)
    bias_part, normed, *early = call(
        bias_kernel,
        [shape((parts, tiles * slots, LANES), BF16), shape((rows * n, C), BF16)]
        + like(flat, ln_gain, ln_shift, w_bias),
        [narrow, pltpu.SemaphoreType.DMA((4,))],
        (flat, ln_gain, ln_shift, w_bias),
        (),
    )
    pair_near, gain_near, shift_near, bias_near = early
    bias_all = exchange(bias_part)
    parted = [
        ((rows * HEADS * n, HD), BF16),
        ((rows * n, HD), BF16),
        ((rows * HEADS * n, 2 * HD), BF16),
        ((rows * n, HD), F32),
    ]
    late = call(
        project_kernel,
        [shape(*each_one) for each_one in parted]
        + [shape((HEADS * n, n), F32)] * 2
        + like(w_qkvg, gate_bias, w_out, out_bias),
        [
            pltpu.SMEM(chain_offset.shape, F32),
            pltpu.VMEM((1, n), jnp.int32),
            pltpu.VMEM((1, n), jnp.int32),
            pltpu.SemaphoreType.DMA((7,)),
        ],
        (chain_offset, mask_row, chain_row, w_qkvg, gate_bias, w_out, out_bias),
        (normed,),
    )
    *projected, known_start, known_end, w_near, gate_near, w_out_near, out_near = late
    sent = call(
        start_kernel,
        shape((parts, square + tiles * slots, LANES), BF16),
        [wide, total, narrow, entries, entries, pltpu.VMEM((rows, HEADS, n), F32)],
        (),
        (
            bias_all, pair_near, *projected, known_start, gain_near, shift_near, bias_near,
            w_out_near, out_near,
        ),
    )
    columns = exchange(sent)
    ended = call(
        end_kernel,
        shape((n * rows, C), BF16),
        [wide, total, entries] + [pltpu.VMEM(*each_one) for each_one in parted],
        (),
        (
            columns, known_end, gain_near, shift_near, w_near, gate_near, w_out_near, out_near
        ),
    )
    return ended.reshape(n, rows, C)


def solution(mesh):
    in_specs = (
        P(("grp", "row", "sub"), None, None),
        P("grp"),
        P("grp"),
        P(),
        P(),
        P(),
        P(),
        P(),
        P(),
        P(),
        P(),
    )
    out_specs = P("grp", ("row", "sub"), None)
    return jax.shard_map(local, mesh=mesh, in_specs=in_specs, out_specs=out_specs, check_vma=False)
```

```python
import functools

import jax
import jax.numpy as jnp
from jax import lax
from jax.experimental import pallas as pl
from jax.experimental.pallas import tpu as pltpu
from jax.sharding import PartitionSpec as P

C = 128
HEADS = 4
HEAD_DIM = 32
HD = 128
LANES = 128
EPS = 1e-05

F32 = jnp.float32
BF16 = jnp.bfloat16
NN = (((1,), (0,)), ((), ()))
NT = (((1,), (1,)), ((), ()))


def matmul(a, b, dims=NN):
    return lax.dot_general(a, b, dims, preferred_element_type=F32)


def layer_norm(values, gain_row, shift_row):
    middle = jnp.mean(values, axis=-1, keepdims=True)
    centred = values - middle
    spread = jnp.mean(jnp.square(centred), axis=-1, keepdims=True)
    return (centred * lax.rsqrt(spread + EPS) * gain_row + shift_row).astype(BF16)


def head_mask(head):
    lane = lax.broadcasted_iota(jnp.int32, (1, HD), 1)
    return jnp.where(lane // HEAD_DIM == head, 1.0, 0.0).astype(F32)


def each(count, unrolled, body):
    if unrolled:
        for index in range(count):
            body(index)
    else:
        lax.fori_loop(0, count, lambda index, _: (body(index), 0)[1], 0)


def block(index, size):
    if isinstance(index, int):
        return slice(index * size, (index + 1) * size)
    return pl.ds(pl.multiple_of(index * size, size), size)


def column_of(row):
    n = row.shape[1]
    first = lax.broadcasted_iota(jnp.int32, (n, n), 0)
    second = lax.broadcasted_iota(jnp.int32, (n, n), 1)
    return jnp.sum(jnp.where(first == second, row, 0.0), axis=1, keepdims=True)


def known_logits(layer, mask, chain, chain_offset, total):
    n = total.shape[1]
    chain_row = chain[...].astype(F32)
    key_row = jnp.where(mask[...] > 0, 0.0, -1000000000.0).astype(F32)
    cross = column_of(chain_row) != chain_row
    for head in range(HEADS):
        total[block(head, n), :] = jnp.where(cross, chain_offset[layer, head], 0.0) + key_row


def add_bias(flip, received, first_slot, wide, known, total):
    n = total.shape[1]
    parts, slots = received.shape[0], wide.shape[0] // received.shape[0]
    for tile in range(n // LANES):
        first = first_slot + tile * slots
        wide[...] = received[:, first : first + slots, :].astype(F32).reshape(parts * slots, LANES)
        span = block(tile, LANES)
        for head in range(HEADS):
            gathered = wide[pl.ds(head, n, stride=HEADS), :]
            if flip:
                here = block(head * (n // LANES) + tile, LANES)
                total[here, :] = gathered.T + known[here, :]
            else:
                here = block(head, n)
                total[here, span] = gathered + known[here, span]


def project(normed, weights, gate_row, queries, keys, values, gates):
    n = normed.shape[0]
    projected = matmul(normed, weights)
    scaled = projected[:, :HD] * (HEAD_DIM ** (-0.5))
    keys[...] = projected[:, HD : 2 * HD].astype(BF16)
    held = projected[:, 2 * HD : 3 * HD]
    gates[...] = jax.nn.sigmoid(projected[:, 3 * HD :].astype(BF16).astype(F32) + gate_row)
    for head in range(HEADS):
        own = head_mask(head)
        queries[block(head, n), :] = (scaled * own).astype(BF16)
        values[block(head, n), :HD] = (held * own).astype(BF16)
        values[block(head, n), HD:] = jnp.broadcast_to(own.astype(BF16), (n, HD))


def attend(queries, keys, values, gates, total):
    n = keys.shape[0]
    logits = matmul(queries[...], keys[...], NT) + total[...]
    expon = jnp.exp(logits - jnp.max(logits, axis=-1, keepdims=True)).astype(BF16)
    beside = jnp.concatenate([expon[block(head, n), :] for head in range(HEADS)], axis=1)
    summed = matmul(beside, values[...])
    return (summed[:, :HD] / summed[:, HD:] * gates[...]).astype(BF16)


def attend_all(queries, keys, values, gates, total, gated):
    n = total.shape[1]

    def step(index):
        here, broad = block(index, n), block(index, HEADS * n)
        gated[here, :] = attend(
            queries.at[broad, :], keys.at[here, :], values.at[broad, :], gates.at[here, :], total
        )

    each(keys.shape[0] // n, n <= LANES, step)


def bias_rows(entries, layer, ln_gain, ln_shift, w_bias, narrow):
    normed = layer_norm(
        entries, ln_gain[layer : layer + 1, :], ln_shift[layer : layer + 1, :]
    )
    bias = matmul(w_bias[layer], normed, NT)
    n = narrow.shape[1]
    for row in range(entries.shape[0] // n):
        narrow[block(row, HEADS), :] = bias[:, block(row, n)]
    return normed


def pack_bias(narrow, first_slot, out):
    parts, (slots, n) = out.shape[0], narrow.shape
    for tile in range(n // LANES):
        part = narrow[:, block(tile, LANES)].astype(BF16)
        first = first_slot + tile * slots
        out[:, first : first + slots, :] = jnp.broadcast_to(part[None], (parts, slots, LANES))


def fetch(pairs, sems):
    copies = [
        pltpu.make_async_copy(far, near, sems.at[index]) for index, (far, near) in enumerate(pairs)
    ]
    for copy in copies:
        copy.start()
    return copies


def bias_kernel(
    pair_far, gain_far, shift_far, bias_far, out, normed_out, pair, ln_gain, ln_shift, w_bias, narrow, sems
):
    far, near = (pair_far, gain_far, shift_far, bias_far), (pair, ln_gain, ln_shift, w_bias)
    for copy in fetch(zip(far, near, strict=True), sems):
        copy.wait()
    normed_out[...] = bias_rows(pair[...].astype(F32), 0, ln_gain, ln_shift, w_bias, narrow)
    pack_bias(narrow, 0, out)


def project_kernel(
    offset_far, mask_far, chain_far, w_far, gate_far, w_out_far, out_bias_far, normed,
    queries, keys, values, gates, known_start, known_end, w_qkvg, gate_bias, w_out, out_bias,
    chain_offset, mask, chain, sems,
):
    n = known_start.shape[1]
    far = (w_far, gate_far, offset_far, mask_far, chain_far, w_out_far, out_bias_far)
    near = (w_qkvg, gate_bias, chain_offset, mask, chain, w_out, out_bias)
    copies = fetch(zip(far, near, strict=True), sems)
    copies[0].wait()
    copies[1].wait()

    def row_step(row):
        here, wide = block(row, n), block(row, HEADS * n)
        project(
            normed[here, :], w_qkvg[0], gate_bias[0:1, :], queries.at[wide, :], keys.at[here, :],
            values.at[wide, :], gates.at[here, :],
        )

    each(keys.shape[0] // n, n <= LANES, row_step)
    for copy in copies[2:]:
        copy.wait()
    known_logits(0, mask, chain, chain_offset, known_start)
    known_logits(1, mask, chain, chain_offset, known_end)


def start_kernel(
    received, pair, queries, keys, values, gates, known, ln_gain, ln_shift, w_bias, w_out, out_bias,
    out, wide, total, gated, narrow, column, packed,
):
    parts, n = out.shape[0], total.shape[1]
    rows = pair.shape[0] // n
    square = rows * rows
    add_bias(False, received, 0, wide, known, total)
    attend_all(queries, keys, values, gates, total, gated)
    update = matmul(gated[...], w_out[0]) + out_bias[0:1, :]
    started = (pair[...].astype(F32) + update).astype(BF16).astype(F32)
    column[...] = started
    bias_rows(started, 1, ln_gain, ln_shift, w_bias, narrow)
    for row in range(rows):
        for place in range(rows):
            packed[pl.ds(row * rows + place, parts, stride=square), :] = column[
                pl.ds(row * n + place, parts, stride=rows), :
            ]
    out[:, :square, :] = packed[...].reshape(parts, square, LANES).astype(BF16)
    pack_bias(narrow, square, out)


def end_kernel(
    received, known, ln_gain, ln_shift, w_qkvg, gate_bias, w_out, out_bias, out, wide, total, gated,
    packed, queries, keys, values, gates,
):
    parts, n = received.shape[0], total.shape[1]
    rows = packed.shape[0] // n
    square = rows * rows
    packed[...] = received[:, :square, :].astype(F32).reshape(parts * square, LANES)

    def project_step(place):
        here, broad = block(place, n), block(place, HEADS * n)
        entries = packed[pl.ds(place, n, stride=rows), :]
        normed = layer_norm(entries, ln_gain[1:2, :], ln_shift[1:2, :])
        project(
            normed, w_qkvg[1], gate_bias[1:2, :], queries.at[broad, :], keys.at[here, :],
            values.at[broad, :], gates.at[here, :],
        )

    each(rows, n <= LANES, project_step)
    add_bias(True, received, square, wide, known, total)
    attend_all(queries, keys, values, gates, total, gated)
    update = matmul(gated[...], w_out[1]) + out_bias[1:2, :]
    for place in range(rows):
        stripe = pl.ds(place, n, stride=rows)
        packed[stripe, :] = packed[stripe, :] + update[block(place, n), :]
    out[...] = packed[...].astype(BF16)


NEAR = pl.BlockSpec(memory_space=pltpu.VMEM)
FAR = pl.BlockSpec(memory_space=pltpu.HBM)


def call(kernel, out_shape, scratch, far, near):
    far = [pltpu.with_memory_space_constraint(array, pltpu.HBM) for array in far]
    return pl.pallas_call(
        kernel,
        out_shape=out_shape,
        in_specs=[FAR] * len(far) + [NEAR] * len(near),
        out_specs=jax.tree.map(lambda _: NEAR, out_shape),
        scratch_shapes=scratch,
        compiler_params=pltpu.CompilerParams(vmem_limit_bytes=40 * 1024 * 1024),
    )(*far, *near)


def local(
    pair, mask, chain, ln_gain, ln_shift, w_qkvg, gate_bias, w_bias, w_out, out_bias, chain_offset
):
    rows, n = pair.shape[0], pair.shape[1]
    parts = lax.axis_size("row") * lax.axis_size("sub")
    tiles, slots, square = n // LANES, rows * HEADS, rows * rows
    exchange = functools.partial(
        lax.all_to_all, axis_name=("row", "sub"), split_axis=0, concat_axis=0, tiled=True
    )
    shape = jax.ShapeDtypeStruct

    def like(*arrays):
        return [shape(array.shape, array.dtype) for array in arrays]

    flat = pair.reshape(rows * n, C)
    mask_row, chain_row = mask.reshape(1, n), chain.reshape(1, n)
    wide = pltpu.VMEM((parts * slots, LANES), F32)
    total = pltpu.VMEM((HEADS * n, n), F32)
    narrow = pltpu.VMEM((slots, n), F32)
    gated = pltpu.VMEM((rows * n, HD), BF16)
    entries = pltpu.VMEM((rows * n, C), F32)
    bias_part, normed, *early = call(
        bias_kernel,
        [shape((parts, tiles * slots, LANES), BF16), shape((rows * n, C), BF16)]
        + like(flat, ln_gain, ln_shift, w_bias),
        [narrow, pltpu.SemaphoreType.DMA((4,))],
        (flat, ln_gain, ln_shift, w_bias),
        (),
    )
    pair_near, gain_near, shift_near, bias_near = early
    bias_all = exchange(bias_part)
    parted = [
        ((rows * HEADS * n, HD), BF16),
        ((rows * n, HD), BF16),
        ((rows * HEADS * n, 2 * HD), BF16),
        ((rows * n, HD), F32),
    ]
    late = call(
        project_kernel,
        [shape(*each_one) for each_one in parted]
        + [shape((HEADS * n, n), F32)] * 2
        + like(w_qkvg, gate_bias, w_out, out_bias),
        [
            pltpu.SMEM(chain_offset.shape, F32),
            pltpu.VMEM((1, n), jnp.int32),
            pltpu.VMEM((1, n), jnp.int32),
            pltpu.SemaphoreType.DMA((7,)),
        ],
        (chain_offset, mask_row, chain_row, w_qkvg, gate_bias, w_out, out_bias),
        (normed,),
    )
    *projected, known_start, known_end, w_near, gate_near, w_out_near, out_near = late
    sent = call(
        start_kernel,
        shape((parts, square + tiles * slots, LANES), BF16),
        [wide, total, gated, narrow, entries, entries],
        (),
        (
            bias_all, pair_near, *projected, known_start, gain_near, shift_near, bias_near,
            w_out_near, out_near,
        ),
    )
    columns = exchange(sent)
    ended = call(
        end_kernel,
        shape((n * rows, C), BF16),
        [wide, total, gated, entries] + [pltpu.VMEM(*each_one) for each_one in parted],
        (),
        (
            columns, known_end, gain_near, shift_near, w_near, gate_near, w_out_near, out_near
        ),
    )
    return ended.reshape(n, rows, C)


def solution(mesh):
    in_specs = (
        P(("grp", "row", "sub"), None, None),
        P("grp"),
        P("grp"),
        P(),
        P(),
        P(),
        P(),
        P(),
        P(),
        P(),
        P(),
    )
    out_specs = P("grp", ("row", "sub"), None)
    return jax.shard_map(local, mesh=mesh, in_specs=in_specs, out_specs=out_specs, check_vma=False)
```

```python
import functools

import jax
import jax.numpy as jnp
from jax import lax
from jax.experimental import pallas as pl
from jax.experimental.pallas import tpu as pltpu
from jax.sharding import PartitionSpec as P

C = 128
HEADS = 4
HEAD_DIM = 32
HD = 128
LANES = 128
EPS = 1e-05

F32 = jnp.float32
BF16 = jnp.bfloat16
NN = (((1,), (0,)), ((), ()))
NT = (((1,), (1,)), ((), ()))


def matmul(a, b, dims=NN):
    return lax.dot_general(a, b, dims, preferred_element_type=F32)


def layer_norm(values, gain_row, shift_row):
    middle = jnp.mean(values, axis=-1, keepdims=True)
    centred = values - middle
    spread = jnp.mean(jnp.square(centred), axis=-1, keepdims=True)
    return (centred * lax.rsqrt(spread + EPS) * gain_row + shift_row).astype(BF16)


def head_mask(head):
    lane = lax.broadcasted_iota(jnp.int32, (1, HD), 1)
    return jnp.where(lane // HEAD_DIM == head, 1.0, 0.0).astype(F32)


def each(count, unrolled, body):
    if unrolled:
        for index in range(count):
            body(index)
    else:
        lax.fori_loop(0, count, lambda index, _: (body(index), 0)[1], 0)


def block(index, size):
    if isinstance(index, int):
        return slice(index * size, (index + 1) * size)
    return pl.ds(pl.multiple_of(index * size, size), size)


def column_of(row):
    n = row.shape[1]
    first = lax.broadcasted_iota(jnp.int32, (n, n), 0)
    second = lax.broadcasted_iota(jnp.int32, (n, n), 1)
    return jnp.sum(jnp.where(first == second, row, 0.0), axis=1, keepdims=True)


def known_logits(layer, mask, chain, chain_offset, total):
    n = total.shape[1]
    chain_row = chain[...].astype(F32)
    key_row = jnp.where(mask[...] > 0, 0.0, -1000000000.0).astype(F32)
    cross = column_of(chain_row) != chain_row
    for head in range(HEADS):
        total[block(head, n), :] = jnp.where(cross, chain_offset[layer, head], 0.0) + key_row


def add_bias(order, received, first_slot, wide, total, known=None):
    n = total.shape[1]
    slots = wide.shape[0] // received.shape[0]
    for tile in range(n // LANES):
        first = first_slot + tile * slots
        for place, part in enumerate(order):
            wide[block(part, slots), :] = received[place, first : first + slots, :].astype(F32)
        span = block(tile, LANES)
        for head in range(HEADS):
            gathered = wide[pl.ds(head, n, stride=HEADS), :]
            if known is not None:
                here = block(head * (n // LANES) + tile, LANES)
                total[here, :] = gathered.T + known[here, :]
            else:
                total[block(head, n), span] = gathered


def project(normed, weights, gate_row, queries, keys, values, gates):
    n = normed.shape[0]
    projected = matmul(normed, weights)
    scaled = projected[:, :HD] * (HEAD_DIM ** (-0.5))
    keys[...] = projected[:, HD : 2 * HD].astype(BF16)
    held = projected[:, 2 * HD : 3 * HD]
    gates[...] = jax.nn.sigmoid(projected[:, 3 * HD :].astype(BF16).astype(F32) + gate_row)
    for head in range(HEADS):
        own = head_mask(head)
        queries[block(head, n), :] = (scaled * own).astype(BF16)
        values[block(head, n), :HD] = (held * own).astype(BF16)
        values[block(head, n), HD:] = jnp.broadcast_to(own.astype(BF16), (n, HD))


def attend(logits, values, gates):
    n = logits.shape[1]
    expon = jnp.exp(logits - jnp.max(logits, axis=-1, keepdims=True)).astype(BF16)
    beside = jnp.concatenate([expon[block(head, n), :] for head in range(HEADS)], axis=1)
    summed = matmul(beside, values)
    return (summed[:, :HD] / summed[:, HD:] * gates).astype(BF16)


def bias_rows(entries, layer, ln_gain, ln_shift, w_bias, narrow):
    normed = layer_norm(
        entries, ln_gain[layer : layer + 1, :], ln_shift[layer : layer + 1, :]
    )
    bias = matmul(w_bias[layer], normed, NT)
    n = narrow.shape[1]
    for row in range(entries.shape[0] // n):
        narrow[block(row, HEADS), :] = bias[:, block(row, n)]
    return normed


def pack_bias(narrow, first_slot, out):
    parts, (slots, n) = out.shape[0], narrow.shape
    for tile in range(n // LANES):
        part = narrow[:, block(tile, LANES)].astype(BF16)
        first = first_slot + tile * slots
        out[:, first : first + slots, :] = jnp.broadcast_to(part[None], (parts, slots, LANES))


def fetch(pairs, sems):
    copies = [
        pltpu.make_async_copy(far, near, sems.at[index]) for index, (far, near) in enumerate(pairs)
    ]
    for copy in copies:
        copy.start()
    return copies


def bias_kernel(
    pair_far, gain_far, shift_far, bias_far, out, normed_out, pair, ln_gain, ln_shift, w_bias, narrow, sems
):
    far, near = (pair_far, gain_far, shift_far, bias_far), (pair, ln_gain, ln_shift, w_bias)
    for copy in fetch(zip(far, near, strict=True), sems):
        copy.wait()
    normed_out[...] = bias_rows(pair[...].astype(F32), 0, ln_gain, ln_shift, w_bias, narrow)
    pack_bias(narrow, 0, out)


def project_kernel(
    offset_far, mask_far, chain_far, w_far, gate_far, w_out_far, out_bias_far, normed,
    logits, values, gates, known_end, w_qkvg, gate_bias, w_out, out_bias,
    chain_offset, mask, chain, known_start, queries, keys, sems,
):
    n = known_start.shape[1]
    far = (w_far, gate_far, offset_far, mask_far, chain_far, w_out_far, out_bias_far)
    near = (w_qkvg, gate_bias, chain_offset, mask, chain, w_out, out_bias)
    copies = fetch(zip(far, near, strict=True), sems)
    for copy in copies:
        copy.wait()
    known_logits(0, mask, chain, chain_offset, known_start)
    known_logits(1, mask, chain, chain_offset, known_end)

    def row_step(row):
        here, wide = block(row, n), block(row, HEADS * n)
        project(
            normed[here, :], w_qkvg[0], gate_bias[0:1, :], queries.at[wide, :], keys.at[here, :],
            values.at[wide, :], gates.at[here, :],
        )
        logits[wide, :] = matmul(queries[wide, :], keys[here, :], NT) + known_start[...]

    each(keys.shape[0] // n, n <= LANES, row_step)


def start_kernel(
    first_order, second_order, received, pair, logits, values, gates, ln_gain, ln_shift, w_bias, w_out,
    out_bias, out, wide, total, gated, narrow, column, packed,
):
    parts, n = out.shape[0], total.shape[1]
    rows = pair.shape[0] // n
    square = rows * rows
    add_bias(first_order, received, 0, wide, total)

    def row_step(row):
        here, broad = block(row, n), block(row, HEADS * n)
        gated[here, :] = attend(logits[broad, :] + total[...], values[broad, :], gates[here, :])

    each(rows, n <= LANES, row_step)
    update = matmul(gated[...], w_out[0]) + out_bias[0:1, :]
    started = (pair[...].astype(F32) + update).astype(BF16).astype(F32)
    column[...] = started
    bias_rows(started, 1, ln_gain, ln_shift, w_bias, narrow)
    for row in range(rows):
        for place in range(rows):
            packed[pl.ds(row * rows + place, parts, stride=square), :] = column[
                pl.ds(row * n + place, parts, stride=rows), :
            ]
    for place, part in enumerate(second_order):
        out[place, :square, :] = packed[block(part, square), :].astype(BF16)
    pack_bias(narrow, square, out)


def end_kernel(
    order, received, known, ln_gain, ln_shift, w_qkvg, gate_bias, w_out, out_bias, out, wide, total, gated,
    packed, queries, keys, values, gates,
):
    parts, n = received.shape[0], total.shape[1]
    rows = packed.shape[0] // n
    square = rows * rows
    for place, part in enumerate(order):
        packed[block(part, square), :] = received[place, :square, :].astype(F32)

    def project_step(place):
        here, broad = block(place, n), block(place, HEADS * n)
        entries = packed[pl.ds(place, n, stride=rows), :]
        normed = layer_norm(entries, ln_gain[1:2, :], ln_shift[1:2, :])
        project(
            normed, w_qkvg[1], gate_bias[1:2, :], queries.at[broad, :], keys.at[here, :],
            values.at[broad, :], gates.at[here, :],
        )

    each(rows, n <= LANES, project_step)
    add_bias(order, received, square, wide, total, known)

    def column_step(place):
        here, broad = block(place, n), block(place, HEADS * n)
        logits = matmul(queries[broad, :], keys[here, :], NT) + total[...]
        gated[here, :] = attend(logits, values[broad, :], gates[here, :])

    each(rows, n <= LANES, column_step)
    update = matmul(gated[...], w_out[1]) + out_bias[1:2, :]
    for place in range(rows):
        stripe = pl.ds(place, n, stride=rows)
        packed[stripe, :] = packed[stripe, :] + update[block(place, n), :]
    out[...] = packed[...].astype(BF16)


NEAR = pl.BlockSpec(memory_space=pltpu.VMEM)
FAR = pl.BlockSpec(memory_space=pltpu.HBM)


def call(kernel, out_shape, scratch, far, near):
    far = [pltpu.with_memory_space_constraint(array, pltpu.HBM) for array in far]
    return pl.pallas_call(
        kernel,
        out_shape=out_shape,
        in_specs=[FAR] * len(far) + [NEAR] * len(near),
        out_specs=jax.tree.map(lambda _: NEAR, out_shape),
        scratch_shapes=scratch,
        compiler_params=pltpu.CompilerParams(vmem_limit_bytes=40 * 1024 * 1024),
    )(*far, *near)


def exchange(array, order):
    return lax.all_to_all(
        array, ("row", "sub"), split_axis=0, concat_axis=0, tiled=True, axis_index_groups=[order]
    )


def orders(outer, inner):
    natural = list(range(outer * inner))
    return natural[::-1], natural


def local(
    pair, mask, chain, ln_gain, ln_shift, w_qkvg, gate_bias, w_bias, w_out, out_bias, chain_offset
):
    rows, n = pair.shape[0], pair.shape[1]
    parts = lax.axis_size("row") * lax.axis_size("sub")
    tiles, slots, square = n // LANES, rows * HEADS, rows * rows
    first_order, second_order = orders(lax.axis_size("row"), lax.axis_size("sub"))
    shape = jax.ShapeDtypeStruct

    def like(*arrays):
        return [shape(array.shape, array.dtype) for array in arrays]

    flat = pair.reshape(rows * n, C)
    mask_row, chain_row = mask.reshape(1, n), chain.reshape(1, n)
    wide = pltpu.VMEM((parts * slots, LANES), F32)
    total = pltpu.VMEM((HEADS * n, n), F32)
    narrow = pltpu.VMEM((slots, n), F32)
    gated = pltpu.VMEM((rows * n, HD), BF16)
    entries = pltpu.VMEM((rows * n, C), F32)
    bias_part, normed, *early = call(
        bias_kernel,
        [shape((parts, tiles * slots, LANES), BF16), shape((rows * n, C), BF16)]
        + like(flat, ln_gain, ln_shift, w_bias),
        [narrow, pltpu.SemaphoreType.DMA((4,))],
        (flat, ln_gain, ln_shift, w_bias),
        (),
    )
    pair_near, gain_near, shift_near, bias_near = early
    bias_all = exchange(bias_part, first_order)
    queries, keys = ((rows * HEADS * n, HD), BF16), ((rows * n, HD), BF16)
    values, gates = ((rows * HEADS * n, 2 * HD), BF16), ((rows * n, HD), F32)
    late = call(
        project_kernel,
        [shape((rows * HEADS * n, n), F32), shape(*values), shape(*gates), shape((HEADS * n, n), F32)]
        + like(w_qkvg, gate_bias, w_out, out_bias),
        [
            pltpu.SMEM(chain_offset.shape, F32),
            pltpu.VMEM((1, n), jnp.int32),
            pltpu.VMEM((1, n), jnp.int32),
            total,
            pltpu.VMEM(*queries),
            pltpu.VMEM(*keys),
            pltpu.SemaphoreType.DMA((7,)),
        ],
        (chain_offset, mask_row, chain_row, w_qkvg, gate_bias, w_out, out_bias),
        (normed,),
    )
    *projected, known_end, w_near, gate_near, w_out_near, out_near = late
    sent = call(
        functools.partial(start_kernel, first_order, second_order),
        shape((parts, square + tiles * slots, LANES), BF16),
        [wide, total, gated, narrow, entries, entries],
        (),
        (
            bias_all, pair_near, *projected, gain_near, shift_near, bias_near, w_out_near, out_near
        ),
    )
    columns = exchange(sent, second_order)
    ended = call(
        functools.partial(end_kernel, second_order),
        shape((n * rows, C), BF16),
        [wide, total, gated, entries] + [pltpu.VMEM(*each_one) for each_one in (queries, keys, values, gates)],
        (),
        (
            columns, known_end, gain_near, shift_near, w_near, gate_near, w_out_near, out_near
        ),
    )
    return ended.reshape(n, rows, C)


def solution(mesh):
    in_specs = (
        P(("grp", "row", "sub"), None, None),
        P("grp"),
        P("grp"),
        P(),
        P(),
        P(),
        P(),
        P(),
        P(),
        P(),
        P(),
    )
    out_specs = P("grp", ("row", "sub"), None)
    return jax.shard_map(local, mesh=mesh, in_specs=in_specs, out_specs=out_specs, check_vma=False)
```

```python
import functools

import jax
import jax.numpy as jnp
from jax import lax
from jax.experimental import pallas as pl
from jax.experimental.pallas import tpu as pltpu
from jax.sharding import PartitionSpec as P

C = 128
HEADS = 4
HEAD_DIM = 32
HD = 128
LANES = 128
EPS = 1e-05

F32 = jnp.float32
BF16 = jnp.bfloat16
NN = (((1,), (0,)), ((), ()))
NT = (((1,), (1,)), ((), ()))


def matmul(a, b, dims=NN):
    return lax.dot_general(a, b, dims, preferred_element_type=F32)


def layer_norm(values, gain_row, shift_row):
    middle = jnp.mean(values, axis=-1, keepdims=True)
    centred = values - middle
    spread = jnp.mean(jnp.square(centred), axis=-1, keepdims=True)
    return (centred * lax.rsqrt(spread + EPS) * gain_row + shift_row).astype(BF16)


def head_mask(head):
    lane = lax.broadcasted_iota(jnp.int32, (1, HD), 1)
    return jnp.where(lane // HEAD_DIM == head, 1.0, 0.0).astype(F32)


def each(count, unrolled, body):
    if unrolled:
        for index in range(count):
            body(index)
    else:
        lax.fori_loop(0, count, lambda index, _: (body(index), 0)[1], 0)


def block(index, size):
    if isinstance(index, int):
        return slice(index * size, (index + 1) * size)
    return pl.ds(pl.multiple_of(index * size, size), size)


def column_of(row):
    n = row.shape[1]
    first = lax.broadcasted_iota(jnp.int32, (n, n), 0)
    second = lax.broadcasted_iota(jnp.int32, (n, n), 1)
    return jnp.sum(jnp.where(first == second, row, 0.0), axis=1, keepdims=True)


def known_logits(layer, mask, chain, chain_offset, total):
    n = total.shape[1]
    chain_row = chain[...].astype(F32)
    key_row = jnp.where(mask[...] > 0, 0.0, -1000000000.0).astype(F32)
    cross = column_of(chain_row) != chain_row
    for head in range(HEADS):
        total[block(head, n), :] = jnp.where(cross, chain_offset[layer, head], 0.0) + key_row


def add_bias(flip, order, received, first_slot, wide, known, total):
    n = total.shape[1]
    slots = wide.shape[0] // received.shape[0]
    for tile in range(n // LANES):
        first = first_slot + tile * slots
        for place, part in enumerate(order):
            wide[block(part, slots), :] = received[place, first : first + slots, :].astype(F32)
        span = block(tile, LANES)
        for head in range(HEADS):
            gathered = wide[pl.ds(head, n, stride=HEADS), :]
            if flip:
                here = block(head * (n // LANES) + tile, LANES)
                total[here, :] = gathered.T + known[here, :]
            else:
                here = block(head, n)
                total[here, span] = gathered + known[here, span]


def project(normed, weights, gate_row, queries, keys, values, gates):
    n = normed.shape[0]
    projected = matmul(normed, weights)
    scaled = projected[:, :HD] * (HEAD_DIM ** (-0.5))
    keys[...] = projected[:, HD : 2 * HD].astype(BF16)
    held = projected[:, 2 * HD : 3 * HD]
    gates[...] = jax.nn.sigmoid(projected[:, 3 * HD :].astype(BF16).astype(F32) + gate_row)
    for head in range(HEADS):
        own = head_mask(head)
        queries[block(head, n), :] = (scaled * own).astype(BF16)
        values[block(head, n), :HD] = (held * own).astype(BF16)
        values[block(head, n), HD:] = jnp.broadcast_to(own.astype(BF16), (n, HD))


def attend(queries, keys, values, gates, total):
    n = keys.shape[0]
    logits = matmul(queries[...], keys[...], NT) + total[...]
    expon = jnp.exp(logits - jnp.max(logits, axis=-1, keepdims=True)).astype(BF16)
    beside = jnp.concatenate([expon[block(head, n), :] for head in range(HEADS)], axis=1)
    summed = matmul(beside, values[...])
    return (summed[:, :HD] / summed[:, HD:] * gates[...]).astype(BF16)


def attend_all(queries, keys, values, gates, total, gated):
    n = total.shape[1]

    def step(index):
        here, broad = block(index, n), block(index, HEADS * n)
        gated[here, :] = attend(
            queries.at[broad, :], keys.at[here, :], values.at[broad, :], gates.at[here, :], total
        )

    each(keys.shape[0] // n, n <= LANES, step)


def bias_rows(entries, layer, ln_gain, ln_shift, w_bias, narrow):
    normed = layer_norm(
        entries, ln_gain[layer : layer + 1, :], ln_shift[layer : layer + 1, :]
    )
    bias = matmul(w_bias[layer], normed, NT)
    n = narrow.shape[1]
    for row in range(entries.shape[0] // n):
        narrow[block(row, HEADS), :] = bias[:, block(row, n)]
    return normed


def pack_bias(narrow, first_slot, out):
    parts, (slots, n) = out.shape[0], narrow.shape
    for tile in range(n // LANES):
        part = narrow[:, block(tile, LANES)].astype(BF16)
        first = first_slot + tile * slots
        out[:, first : first + slots, :] = jnp.broadcast_to(part[None], (parts, slots, LANES))


def fetch(pairs, sems):
    copies = [
        pltpu.make_async_copy(far, near, sems.at[index]) for index, (far, near) in enumerate(pairs)
    ]
    for copy in copies:
        copy.start()
    return copies


def bias_kernel(
    pair_far, mask_far, chain_far, offset_far, gain_far, shift_far, bias_far, gate_far, out_far,
    w_qkvg_far, w_out_far,
    out, normed, known_start, known_end, pair, ln_gain, ln_shift, w_bias, gate_bias, out_bias, w_qkvg, w_out,
    mask, chain, chain_offset, narrow, sems,
):
    moves = (
        (pair_far, pair), (mask_far, mask), (chain_far, chain), (offset_far, chain_offset),
        (gain_far, ln_gain), (shift_far, ln_shift), (bias_far, w_bias), (gate_far, gate_bias),
        (out_far, out_bias), (w_qkvg_far, w_qkvg), (w_out_far, w_out),
    )
    copies = [
        pltpu.make_async_copy(far, near, sems.at[index]) for index, (far, near) in enumerate(moves)
    ]
    for copy in copies:
        copy.start()
    for copy in copies[1:7]:
        copy.wait()
    known_logits(0, mask, chain, chain_offset, known_start)
    known_logits(1, mask, chain, chain_offset, known_end)
    copies[0].wait()
    normed[...] = bias_rows(pair[...].astype(F32), 0, ln_gain, ln_shift, w_bias, narrow)
    pack_bias(narrow, 0, out)
    for copy in copies[7:]:
        copy.wait()


def start_kernel(
    first_order, second_order, received, normed, pair, known, ln_gain, ln_shift, w_bias, gate_bias,
    out_bias, w_qkvg, w_out, out, wide, total, gated, narrow, column, packed, queries, keys, values, gates,
):
    parts, n = out.shape[0], total.shape[1]
    rows = pair.shape[0] // n
    square = rows * rows

    def project_step(row):
        here, broad = block(row, n), block(row, HEADS * n)
        project(
            normed[here, :], w_qkvg[0], gate_bias[0:1, :], queries.at[broad, :], keys.at[here, :],
            values.at[broad, :], gates.at[here, :],
        )

    each(rows, n <= LANES, project_step)
    add_bias(False, first_order, received, 0, wide, known, total)
    attend_all(queries, keys, values, gates, total, gated)
    update = matmul(gated[...], w_out[0]) + out_bias[0:1, :]
    started = (pair[...].astype(F32) + update).astype(BF16).astype(F32)
    column[...] = started
    bias_rows(started, 1, ln_gain, ln_shift, w_bias, narrow)
    for row in range(rows):
        for place in range(rows):
            packed[pl.ds(row * rows + place, parts, stride=square), :] = column[
                pl.ds(row * n + place, parts, stride=rows), :
            ]
    for place, part in enumerate(second_order):
        out[place, :square, :] = packed[block(part, square), :].astype(BF16)
    pack_bias(narrow, square, out)


def end_kernel(
    order, received, known, ln_gain, ln_shift, gate_bias, out_bias, w_qkvg, w_out, out, wide, total, gated,
    packed, queries, keys, values, gates,
):
    n = total.shape[1]
    rows = packed.shape[0] // n
    square = rows * rows
    for place, part in enumerate(order):
        packed[block(part, square), :] = received[place, :square, :].astype(F32)

    def project_step(place):
        here, broad = block(place, n), block(place, HEADS * n)
        entries = packed[pl.ds(place, n, stride=rows), :]
        normed = layer_norm(entries, ln_gain[1:2, :], ln_shift[1:2, :])
        project(
            normed, w_qkvg[1], gate_bias[1:2, :], queries.at[broad, :], keys.at[here, :],
            values.at[broad, :], gates.at[here, :],
        )

    each(rows, n <= LANES, project_step)
    add_bias(True, order, received, square, wide, known, total)
    attend_all(queries, keys, values, gates, total, gated)
    update = matmul(gated[...], w_out[1]) + out_bias[1:2, :]
    for place in range(rows):
        stripe = pl.ds(place, n, stride=rows)
        packed[stripe, :] = packed[stripe, :] + update[block(place, n), :]
    out[...] = packed[...].astype(BF16)


NEAR = pl.BlockSpec(memory_space=pltpu.VMEM)
FAR = pl.BlockSpec(memory_space=pltpu.HBM)


def call(kernel, out_shape, scratch, far, near):
    far = [pltpu.with_memory_space_constraint(array, pltpu.HBM) for array in far]
    return pl.pallas_call(
        kernel,
        out_shape=out_shape,
        in_specs=[FAR] * len(far) + [NEAR] * len(near),
        out_specs=jax.tree.map(lambda _: NEAR, out_shape),
        scratch_shapes=scratch,
        compiler_params=pltpu.CompilerParams(vmem_limit_bytes=40 * 1024 * 1024),
    )(*far, *near)


def exchange(array, order):
    return lax.all_to_all(
        array, ("row", "sub"), split_axis=0, concat_axis=0, tiled=True, axis_index_groups=[order]
    )


def orders(outer, inner):
    natural = list(range(outer * inner))
    return natural[::-1], natural


def local(
    pair, mask, chain, ln_gain, ln_shift, w_qkvg, gate_bias, w_bias, w_out, out_bias, chain_offset
):
    rows, n = pair.shape[0], pair.shape[1]
    parts = lax.axis_size("row") * lax.axis_size("sub")
    tiles, slots, square = n // LANES, rows * HEADS, rows * rows
    first_order, second_order = orders(lax.axis_size("row"), lax.axis_size("sub"))
    shape = jax.ShapeDtypeStruct

    def like(*arrays):
        return [shape(array.shape, array.dtype) for array in arrays]

    flat = pair.reshape(rows * n, C)
    mask_row, chain_row = mask.reshape(1, n), chain.reshape(1, n)
    wide = pltpu.VMEM((parts * slots, LANES), F32)
    total = pltpu.VMEM((HEADS * n, n), F32)
    narrow = pltpu.VMEM((slots, n), F32)
    gated = pltpu.VMEM((rows * n, HD), BF16)
    entries = pltpu.VMEM((rows * n, C), F32)
    parted = [
        pltpu.VMEM((rows * HEADS * n, HD), BF16),
        pltpu.VMEM((rows * n, HD), BF16),
        pltpu.VMEM((rows * HEADS * n, 2 * HD), BF16),
        pltpu.VMEM((rows * n, HD), F32),
    ]
    known = shape((HEADS * n, n), F32)
    kept = (ln_gain, ln_shift, w_bias, gate_bias, out_bias, w_qkvg, w_out)
    bias_part, normed, known_start, known_end, pair_near, *near = call(
        bias_kernel,
        [shape((parts, tiles * slots, LANES), BF16), shape((rows * n, C), BF16), known, known]
        + like(flat, *kept),
        [
            pltpu.VMEM((1, n), jnp.int32),
            pltpu.VMEM((1, n), jnp.int32),
            pltpu.SMEM(chain_offset.shape, F32),
            narrow,
            pltpu.SemaphoreType.DMA((11,)),
        ],
        (flat, mask_row, chain_row, chain_offset, *kept),
        (),
    )
    bias_all = exchange(bias_part, first_order)
    sent = call(
        functools.partial(start_kernel, first_order, second_order),
        shape((parts, square + tiles * slots, LANES), BF16),
        [wide, total, gated, narrow, entries, entries, *parted],
        (),
        (bias_all, normed, pair_near, known_start, *near),
    )
    columns = exchange(sent, second_order)
    gain_near, shift_near, _, *near = near
    ended = call(
        functools.partial(end_kernel, second_order),
        shape((n * rows, C), BF16),
        [wide, total, gated, entries, *parted],
        (),
        (columns, known_end, gain_near, shift_near, *near),
    )
    return ended.reshape(n, rows, C)


def solution(mesh):
    in_specs = (
        P(("grp", "row", "sub"), None, None),
        P("grp"),
        P("grp"),
        P(),
        P(),
        P(),
        P(),
        P(),
        P(),
        P(),
        P(),
    )
    out_specs = P("grp", ("row", "sub"), None)
    return jax.shard_map(local, mesh=mesh, in_specs=in_specs, out_specs=out_specs, check_vma=False)
```

```python
import functools

import jax
import jax.numpy as jnp
from jax import lax
from jax.experimental import pallas as pl
from jax.experimental.pallas import tpu as pltpu
from jax.sharding import PartitionSpec as P

C = 128
HEADS = 4
HEAD_DIM = 32
HD = 128
LANES = 128
EPS = 1e-05

F32 = jnp.float32
BF16 = jnp.bfloat16
NN = (((1,), (0,)), ((), ()))
NT = (((1,), (1,)), ((), ()))


def matmul(a, b, dims=NN):
    return lax.dot_general(a, b, dims, preferred_element_type=F32)


def layer_norm(values, gain_row, shift_row):
    middle = jnp.mean(values, axis=-1, keepdims=True)
    centred = values - middle
    spread = jnp.mean(jnp.square(centred), axis=-1, keepdims=True)
    return (centred * lax.rsqrt(spread + EPS) * gain_row + shift_row).astype(BF16)


def head_mask(head):
    lane = lax.broadcasted_iota(jnp.int32, (1, HD), 1)
    return jnp.where(lane // HEAD_DIM == head, 1.0, 0.0).astype(BF16)


def each(count, unrolled, body):
    if unrolled:
        for index in range(count):
            body(index)
    else:
        lax.fori_loop(0, count, lambda index, _: (body(index), 0)[1], 0)


def block(index, size):
    if isinstance(index, int):
        return slice(index * size, (index + 1) * size)
    return pl.ds(pl.multiple_of(index * size, size), size)


def column_of(row):
    n = row.shape[1]
    first = lax.broadcasted_iota(jnp.int32, (n, n), 0)
    second = lax.broadcasted_iota(jnp.int32, (n, n), 1)
    return jnp.sum(jnp.where(first == second, row, 0.0), axis=1, keepdims=True)


def known_logits(layer, mask, chain, chain_offset, total):
    n = total.shape[1]
    chain_row = chain[...].astype(F32)
    key_row = jnp.where(mask[...] > 0, 0.0, -1000000000.0).astype(F32)
    cross = column_of(chain_row) != chain_row
    for head in range(HEADS):
        total[block(head, n), :] = jnp.where(cross, chain_offset[layer, head], 0.0) + key_row


def add_bias(flip, order, received, first_slot, wide, known, total):
    n = total.shape[1]
    slots = wide.shape[0] // received.shape[0]
    for tile in range(n // LANES):
        first = first_slot + tile * slots
        for place, part in enumerate(order):
            wide[block(part, slots), :] = received[place, first : first + slots, :].astype(F32)
        span = block(tile, LANES)
        for head in range(HEADS):
            gathered = wide[pl.ds(head, n, stride=HEADS), :]
            if flip:
                here = block(head * (n // LANES) + tile, LANES)
                total[here, :] = gathered.T + known[here, :]
            else:
                here = block(head, n)
                total[here, span] = gathered + known[here, span]


def project(normed, weights, gate_row, queries, keys, values, gates):
    n = normed.shape[0]
    projected = matmul(normed, weights)
    scaled = (projected[:, :HD] * (HEAD_DIM ** (-0.5))).astype(BF16)
    keys[...] = projected[:, HD : 2 * HD].astype(BF16)
    held = projected[:, 2 * HD : 3 * HD].astype(BF16)
    gates[...] = jax.nn.sigmoid(projected[:, 3 * HD :].astype(BF16).astype(F32) + gate_row)
    for head in range(HEADS):
        own = head_mask(head)
        queries[block(head, n), :] = scaled * own
        values[block(head, n), :HD] = held * own
        values[block(head, n), HD:] = jnp.broadcast_to(own, (n, HD))


def attend(queries, keys, values, gates, total):
    n = keys.shape[0]
    logits = matmul(queries[...], keys[...], NT) + total[...]
    expon = jnp.exp(logits - jnp.max(logits, axis=-1, keepdims=True)).astype(BF16)
    beside = jnp.concatenate([expon[block(head, n), :] for head in range(HEADS)], axis=1)
    summed = matmul(beside, values[...])
    return (summed[:, :HD] / summed[:, HD:] * gates[...]).astype(BF16)


def attend_all(queries, keys, values, gates, total, gated):
    n = total.shape[1]

    def step(index):
        here, broad = block(index, n), block(index, HEADS * n)
        gated[here, :] = attend(
            queries.at[broad, :], keys.at[here, :], values.at[broad, :], gates.at[here, :], total
        )

    each(keys.shape[0] // n, n <= LANES, step)


def bias_rows(entries, layer, ln_gain, ln_shift, w_bias, narrow):
    normed = layer_norm(
        entries, ln_gain[layer : layer + 1, :], ln_shift[layer : layer + 1, :]
    )
    bias = matmul(w_bias[layer], normed, NT)
    n = narrow.shape[1]
    for row in range(entries.shape[0] // n):
        narrow[block(row, HEADS), :] = bias[:, block(row, n)]
    return normed


def pack_bias(narrow, first_slot, out):
    parts, (slots, n) = out.shape[0], narrow.shape
    for tile in range(n // LANES):
        part = narrow[:, block(tile, LANES)].astype(BF16)
        first = first_slot + tile * slots
        out[:, first : first + slots, :] = jnp.broadcast_to(part[None], (parts, slots, LANES))


def fetch(pairs, sems):
    copies = [
        pltpu.make_async_copy(far, near, sems.at[index]) for index, (far, near) in enumerate(pairs)
    ]
    for copy in copies:
        copy.start()
    return copies


def bias_kernel(
    pair_far, mask_far, chain_far, offset_far, gain_far, shift_far, bias_far, gate_far, out_far,
    w_qkvg_far, w_out_far,
    out, normed, known_start, known_end, pair, ln_gain, ln_shift, w_bias, gate_bias, out_bias, w_qkvg, w_out,
    mask, chain, chain_offset, narrow, sems,
):
    moves = (
        (pair_far, pair), (mask_far, mask), (chain_far, chain), (offset_far, chain_offset),
        (gain_far, ln_gain), (shift_far, ln_shift), (bias_far, w_bias), (gate_far, gate_bias),
        (out_far, out_bias), (w_qkvg_far, w_qkvg), (w_out_far, w_out),
    )
    copies = [
        pltpu.make_async_copy(far, near, sems.at[index]) for index, (far, near) in enumerate(moves)
    ]
    for copy in copies:
        copy.start()
    for copy in copies[1:7]:
        copy.wait()
    known_logits(0, mask, chain, chain_offset, known_start)
    known_logits(1, mask, chain, chain_offset, known_end)
    copies[0].wait()
    normed[...] = bias_rows(pair[...].astype(F32), 0, ln_gain, ln_shift, w_bias, narrow)
    pack_bias(narrow, 0, out)
    for copy in copies[7:]:
        copy.wait()


def start_kernel(
    first_order, second_order, received, normed, pair, known, ln_gain, ln_shift, w_bias, gate_bias,
    out_bias, w_qkvg, w_out, out, wide, total, gated, narrow, column, packed, queries, keys, values, gates,
):
    parts, n = out.shape[0], total.shape[1]
    rows = pair.shape[0] // n
    square = rows * rows

    def project_step(row):
        here, broad = block(row, n), block(row, HEADS * n)
        project(
            normed[here, :], w_qkvg[0], gate_bias[0:1, :], queries.at[broad, :], keys.at[here, :],
            values.at[broad, :], gates.at[here, :],
        )

    each(rows, n <= LANES, project_step)
    add_bias(False, first_order, received, 0, wide, known, total)
    attend_all(queries, keys, values, gates, total, gated)
    update = matmul(gated[...], w_out[0]) + out_bias[0:1, :]
    started = (pair[...].astype(F32) + update).astype(BF16).astype(F32)
    column[...] = started
    bias_rows(started, 1, ln_gain, ln_shift, w_bias, narrow)
    for row in range(rows):
        for place in range(rows):
            packed[pl.ds(row * rows + place, parts, stride=square), :] = column[
                pl.ds(row * n + place, parts, stride=rows), :
            ]
    for place, part in enumerate(second_order):
        out[place, :square, :] = packed[block(part, square), :].astype(BF16)
    pack_bias(narrow, square, out)


def end_kernel(
    order, received, known, ln_gain, ln_shift, gate_bias, out_bias, w_qkvg, w_out, out, wide, total, gated,
    packed, queries, keys, values, gates,
):
    n = total.shape[1]
    rows = packed.shape[0] // n
    square = rows * rows
    for place, part in enumerate(order):
        packed[block(part, square), :] = received[place, :square, :].astype(F32)

    def project_step(place):
        here, broad = block(place, n), block(place, HEADS * n)
        entries = packed[pl.ds(place, n, stride=rows), :]
        normed = layer_norm(entries, ln_gain[1:2, :], ln_shift[1:2, :])
        project(
            normed, w_qkvg[1], gate_bias[1:2, :], queries.at[broad, :], keys.at[here, :],
            values.at[broad, :], gates.at[here, :],
        )

    each(rows, n <= LANES, project_step)
    add_bias(True, order, received, square, wide, known, total)
    attend_all(queries, keys, values, gates, total, gated)
    update = matmul(gated[...], w_out[1]) + out_bias[1:2, :]
    for place in range(rows):
        stripe = pl.ds(place, n, stride=rows)
        packed[stripe, :] = packed[stripe, :] + update[block(place, n), :]
    out[...] = packed[...].astype(BF16)


NEAR = pl.BlockSpec(memory_space=pltpu.VMEM)
FAR = pl.BlockSpec(memory_space=pltpu.HBM)


def call(kernel, out_shape, scratch, far, near):
    far = [pltpu.with_memory_space_constraint(array, pltpu.HBM) for array in far]
    return pl.pallas_call(
        kernel,
        out_shape=out_shape,
        in_specs=[FAR] * len(far) + [NEAR] * len(near),
        out_specs=jax.tree.map(lambda _: NEAR, out_shape),
        scratch_shapes=scratch,
        compiler_params=pltpu.CompilerParams(vmem_limit_bytes=40 * 1024 * 1024),
    )(*far, *near)


def exchange(array, order):
    return lax.all_to_all(
        array, ("row", "sub"), split_axis=0, concat_axis=0, tiled=True, axis_index_groups=[order]
    )


def orders(outer, inner):
    natural = list(range(outer * inner))
    pair = 2 if outer % 2 == 0 else 1
    apart = [
        (place * pair + half) * inner + part
        for half in range(pair)
        for part in range(inner)
        for place in range(outer // pair)
    ]
    return natural[::-1], apart[::-1]


def local(
    pair, mask, chain, ln_gain, ln_shift, w_qkvg, gate_bias, w_bias, w_out, out_bias, chain_offset
):
    rows, n = pair.shape[0], pair.shape[1]
    parts = lax.axis_size("row") * lax.axis_size("sub")
    tiles, slots, square = n // LANES, rows * HEADS, rows * rows
    first_order, second_order = orders(lax.axis_size("row"), lax.axis_size("sub"))
    shape = jax.ShapeDtypeStruct

    def like(*arrays):
        return [shape(array.shape, array.dtype) for array in arrays]

    flat = pair.reshape(rows * n, C)
    mask_row, chain_row = mask.reshape(1, n), chain.reshape(1, n)
    wide = pltpu.VMEM((parts * slots, LANES), F32)
    total = pltpu.VMEM((HEADS * n, n), F32)
    narrow = pltpu.VMEM((slots, n), F32)
    gated = pltpu.VMEM((rows * n, HD), BF16)
    entries = pltpu.VMEM((rows * n, C), F32)
    parted = [
        pltpu.VMEM((rows * HEADS * n, HD), BF16),
        pltpu.VMEM((rows * n, HD), BF16),
        pltpu.VMEM((rows * HEADS * n, 2 * HD), BF16),
        pltpu.VMEM((rows * n, HD), F32),
    ]
    known = shape((HEADS * n, n), F32)
    kept = (ln_gain, ln_shift, w_bias, gate_bias, out_bias, w_qkvg, w_out)
    bias_part, normed, known_start, known_end, pair_near, *near = call(
        bias_kernel,
        [shape((parts, tiles * slots, LANES), BF16), shape((rows * n, C), BF16), known, known]
        + like(flat, *kept),
        [
            pltpu.VMEM((1, n), jnp.int32),
            pltpu.VMEM((1, n), jnp.int32),
            pltpu.SMEM(chain_offset.shape, F32),
            narrow,
            pltpu.SemaphoreType.DMA((11,)),
        ],
        (flat, mask_row, chain_row, chain_offset, *kept),
        (),
    )
    bias_all = exchange(bias_part, first_order)
    sent = call(
        functools.partial(start_kernel, first_order, second_order),
        shape((parts, square + tiles * slots, LANES), BF16),
        [wide, total, gated, narrow, entries, entries, *parted],
        (),
        (bias_all, normed, pair_near, known_start, *near),
    )
    columns = exchange(sent, second_order)
    gain_near, shift_near, _, *near = near
    ended = call(
        functools.partial(end_kernel, second_order),
        shape((n * rows, C), BF16),
        [wide, total, gated, entries, *parted],
        (),
        (columns, known_end, gain_near, shift_near, *near),
    )
    return ended.reshape(n, rows, C)


def solution(mesh):
    in_specs = (
        P(("grp", "row", "sub"), None, None),
        P("grp"),
        P("grp"),
        P(),
        P(),
        P(),
        P(),
        P(),
        P(),
        P(),
        P(),
    )
    out_specs = P("grp", ("row", "sub"), None)
    return jax.shard_map(local, mesh=mesh, in_specs=in_specs, out_specs=out_specs, check_vma=False)
```

```python
import functools

import jax
import jax.numpy as jnp
from jax import lax
from jax.experimental import pallas as pl
from jax.experimental.pallas import tpu as pltpu
from jax.sharding import PartitionSpec as P

C = 128
HEADS = 4
HEAD_DIM = 32
HD = 128
LANES = 128
EPS = 1e-05

F32 = jnp.float32
BF16 = jnp.bfloat16
NN = (((1,), (0,)), ((), ()))
NT = (((1,), (1,)), ((), ()))


def matmul(a, b, dims=NN):
    return lax.dot_general(a, b, dims, preferred_element_type=F32)


def layer_norm(values, gain_row, shift_row):
    middle = jnp.mean(values, axis=-1, keepdims=True)
    centred = values - middle
    spread = jnp.mean(jnp.square(centred), axis=-1, keepdims=True)
    return (centred * lax.rsqrt(spread + EPS) * gain_row + shift_row).astype(BF16)


def head_mask(head):
    lane = lax.broadcasted_iota(jnp.int32, (1, HD), 1)
    return jnp.where(lane // HEAD_DIM == head, 1.0, 0.0).astype(BF16)


def each(count, unrolled, body):
    if unrolled:
        for index in range(count):
            body(index)
    else:
        lax.fori_loop(0, count, lambda index, _: (body(index), 0)[1], 0)


def block(index, size):
    if isinstance(index, int):
        return slice(index * size, (index + 1) * size)
    return pl.ds(pl.multiple_of(index * size, size), size)


def column_of(row):
    n = row.shape[1]
    first = lax.broadcasted_iota(jnp.int32, (n, n), 0)
    second = lax.broadcasted_iota(jnp.int32, (n, n), 1)
    return jnp.sum(jnp.where(first == second, row, 0.0), axis=1, keepdims=True)


def known_logits(layer, mask, chain, chain_offset, total):
    n = total.shape[1]
    chain_row = chain[...].astype(F32)
    key_row = jnp.where(mask[...] > 0, 0.0, -1000000000.0).astype(F32)
    cross = column_of(chain_row) != chain_row
    for head in range(HEADS):
        total[block(head, n), :] = jnp.where(cross, chain_offset[layer, head], 0.0) + key_row


def add_bias(flip, order, received, first_slot, wide, known, total):
    n = total.shape[1]
    slots = wide.shape[0] // received.shape[0]
    for tile in range(n // LANES):
        first = first_slot + tile * slots
        for place, part in enumerate(order):
            wide[block(part, slots), :] = received[place, first : first + slots, :].astype(F32)
        span = block(tile, LANES)
        for head in range(HEADS):
            gathered = wide[pl.ds(head, n, stride=HEADS), :]
            if flip:
                here = block(head * (n // LANES) + tile, LANES)
                total[here, :] = gathered.T + known[here, :]
            else:
                here = block(head, n)
                total[here, span] = gathered + known[here, span]


def project(normed, weights, gate_row, queries, keys, values, gates):
    n = normed.shape[0]
    projected = matmul(normed, weights)
    scaled = (projected[:, :HD] * (HEAD_DIM ** (-0.5))).astype(BF16)
    keys[...] = projected[:, HD : 2 * HD].astype(BF16)
    held = projected[:, 2 * HD : 3 * HD].astype(BF16)
    gates[...] = jax.nn.sigmoid(projected[:, 3 * HD :].astype(BF16).astype(F32) + gate_row)
    for head in range(HEADS):
        own = head_mask(head)
        queries[block(head, n), :] = scaled * own
        values[block(head, n), :] = held * own


def attend(queries, keys, values, gates, total):
    n = keys.shape[0]
    logits = matmul(queries[...], keys[...], NT) + total[...]
    expon = jnp.exp(logits - jnp.max(logits, axis=-1, keepdims=True))
    weights = (expon / jnp.sum(expon, axis=-1, keepdims=True)).astype(BF16)
    beside = jnp.concatenate([weights[block(head, n), :] for head in range(HEADS)], axis=1)
    summed = matmul(beside, values[...])
    return (summed * gates[...]).astype(BF16)


def attend_all(queries, keys, values, gates, total, gated):
    n = total.shape[1]

    def step(index):
        here, broad = block(index, n), block(index, HEADS * n)
        gated[here, :] = attend(
            queries.at[broad, :], keys.at[here, :], values.at[broad, :], gates.at[here, :], total
        )

    each(keys.shape[0] // n, n <= LANES, step)


def bias_rows(entries, layer, ln_gain, ln_shift, w_bias, narrow):
    normed = layer_norm(
        entries, ln_gain[layer : layer + 1, :], ln_shift[layer : layer + 1, :]
    )
    bias = matmul(w_bias[layer], normed, NT)
    n = narrow.shape[1]
    for row in range(entries.shape[0] // n):
        narrow[block(row, HEADS), :] = bias[:, block(row, n)]
    return normed


def pack_bias(narrow, first_slot, out):
    parts, (slots, n) = out.shape[0], narrow.shape
    for tile in range(n // LANES):
        part = narrow[:, block(tile, LANES)].astype(BF16)
        first = first_slot + tile * slots
        out[:, first : first + slots, :] = jnp.broadcast_to(part[None], (parts, slots, LANES))


def fetch(pairs, sems):
    copies = [
        pltpu.make_async_copy(far, near, sems.at[index]) for index, (far, near) in enumerate(pairs)
    ]
    for copy in copies:
        copy.start()
    return copies


def bias_kernel(
    pair_far, mask_far, chain_far, offset_far, gain_far, shift_far, bias_far, gate_far, out_far,
    w_qkvg_far, w_out_far,
    out, normed, known_start, known_end, pair, ln_gain, ln_shift, w_bias, gate_bias, out_bias, w_qkvg, w_out,
    mask, chain, chain_offset, narrow, sems,
):
    moves = (
        (pair_far, pair), (mask_far, mask), (chain_far, chain), (offset_far, chain_offset),
        (gain_far, ln_gain), (shift_far, ln_shift), (bias_far, w_bias), (gate_far, gate_bias),
        (out_far, out_bias), (w_qkvg_far, w_qkvg), (w_out_far, w_out),
    )
    copies = [
        pltpu.make_async_copy(far, near, sems.at[index]) for index, (far, near) in enumerate(moves)
    ]
    for copy in copies:
        copy.start()
    for copy in copies[1:7]:
        copy.wait()
    known_logits(0, mask, chain, chain_offset, known_start)
    known_logits(1, mask, chain, chain_offset, known_end)
    copies[0].wait()
    normed[...] = bias_rows(pair[...].astype(F32), 0, ln_gain, ln_shift, w_bias, narrow)
    pack_bias(narrow, 0, out)
    for copy in copies[7:]:
        copy.wait()


def start_kernel(
    first_order, second_order, received, normed, pair, known, ln_gain, ln_shift, w_bias, gate_bias,
    out_bias, w_qkvg, w_out, out, wide, total, gated, narrow, column, packed, queries, keys, values, gates,
):
    parts, n = out.shape[0], total.shape[1]
    rows = pair.shape[0] // n
    square = rows * rows

    def project_step(row):
        here, broad = block(row, n), block(row, HEADS * n)
        project(
            normed[here, :], w_qkvg[0], gate_bias[0:1, :], queries.at[broad, :], keys.at[here, :],
            values.at[broad, :], gates.at[here, :],
        )

    each(rows, n <= LANES, project_step)
    add_bias(False, first_order, received, 0, wide, known, total)
    attend_all(queries, keys, values, gates, total, gated)
    update = matmul(gated[...], w_out[0]) + out_bias[0:1, :]
    started = (pair[...].astype(F32) + update).astype(BF16).astype(F32)
    column[...] = started
    bias_rows(started, 1, ln_gain, ln_shift, w_bias, narrow)
    for row in range(rows):
        for place in range(rows):
            packed[pl.ds(row * rows + place, parts, stride=square), :] = column[
                pl.ds(row * n + place, parts, stride=rows), :
            ]
    for place, part in enumerate(second_order):
        out[place, :square, :] = packed[block(part, square), :].astype(BF16)
    pack_bias(narrow, square, out)


def end_kernel(
    order, received, known, ln_gain, ln_shift, gate_bias, out_bias, w_qkvg, w_out, out, wide, total, gated,
    packed, queries, keys, values, gates,
):
    n = total.shape[1]
    rows = packed.shape[0] // n
    square = rows * rows
    for place, part in enumerate(order):
        packed[block(part, square), :] = received[place, :square, :].astype(F32)

    def project_step(place):
        here, broad = block(place, n), block(place, HEADS * n)
        entries = packed[pl.ds(place, n, stride=rows), :]
        normed = layer_norm(entries, ln_gain[1:2, :], ln_shift[1:2, :])
        project(
            normed, w_qkvg[1], gate_bias[1:2, :], queries.at[broad, :], keys.at[here, :],
            values.at[broad, :], gates.at[here, :],
        )

    each(rows, n <= LANES, project_step)
    add_bias(True, order, received, square, wide, known, total)
    attend_all(queries, keys, values, gates, total, gated)
    update = matmul(gated[...], w_out[1]) + out_bias[1:2, :]
    for place in range(rows):
        stripe = pl.ds(place, n, stride=rows)
        packed[stripe, :] = packed[stripe, :] + update[block(place, n), :]
    out[...] = packed[...].astype(BF16)


NEAR = pl.BlockSpec(memory_space=pltpu.VMEM)
FAR = pl.BlockSpec(memory_space=pltpu.HBM)


def call(kernel, out_shape, scratch, far, near):
    far = [pltpu.with_memory_space_constraint(array, pltpu.HBM) for array in far]
    return pl.pallas_call(
        kernel,
        out_shape=out_shape,
        in_specs=[FAR] * len(far) + [NEAR] * len(near),
        out_specs=jax.tree.map(lambda _: NEAR, out_shape),
        scratch_shapes=scratch,
        compiler_params=pltpu.CompilerParams(vmem_limit_bytes=40 * 1024 * 1024),
    )(*far, *near)


def exchange(array, order):
    return lax.all_to_all(
        array, ("row", "sub"), split_axis=0, concat_axis=0, tiled=True, axis_index_groups=[order]
    )


def orders(outer, inner):
    natural = list(range(outer * inner))
    pair = 2 if outer % 2 == 0 else 1
    apart = [
        (place * pair + half) * inner + part
        for half in range(pair)
        for part in range(inner)
        for place in range(outer // pair)
    ]
    return natural[::-1], apart[::-1]


def local(
    pair, mask, chain, ln_gain, ln_shift, w_qkvg, gate_bias, w_bias, w_out, out_bias, chain_offset
):
    rows, n = pair.shape[0], pair.shape[1]
    parts = lax.axis_size("row") * lax.axis_size("sub")
    tiles, slots, square = n // LANES, rows * HEADS, rows * rows
    first_order, second_order = orders(lax.axis_size("row"), lax.axis_size("sub"))
    shape = jax.ShapeDtypeStruct

    def like(*arrays):
        return [shape(array.shape, array.dtype) for array in arrays]

    flat = pair.reshape(rows * n, C)
    mask_row, chain_row = mask.reshape(1, n), chain.reshape(1, n)
    wide = pltpu.VMEM((parts * slots, LANES), F32)
    total = pltpu.VMEM((HEADS * n, n), F32)
    narrow = pltpu.VMEM((slots, n), F32)
    gated = pltpu.VMEM((rows * n, HD), BF16)
    entries = pltpu.VMEM((rows * n, C), F32)
    parted = [
        pltpu.VMEM((rows * HEADS * n, HD), BF16),
        pltpu.VMEM((rows * n, HD), BF16),
        pltpu.VMEM((rows * HEADS * n, HD), BF16),
        pltpu.VMEM((rows * n, HD), F32),
    ]
    known = shape((HEADS * n, n), F32)
    kept = (ln_gain, ln_shift, w_bias, gate_bias, out_bias, w_qkvg, w_out)
    bias_part, normed, known_start, known_end, pair_near, *near = call(
        bias_kernel,
        [shape((parts, tiles * slots, LANES), BF16), shape((rows * n, C), BF16), known, known]
        + like(flat, *kept),
        [
            pltpu.VMEM((1, n), jnp.int32),
            pltpu.VMEM((1, n), jnp.int32),
            pltpu.SMEM(chain_offset.shape, F32),
            narrow,
            pltpu.SemaphoreType.DMA((11,)),
        ],
        (flat, mask_row, chain_row, chain_offset, *kept),
        (),
    )
    bias_all = exchange(bias_part, first_order)
    sent = call(
        functools.partial(start_kernel, first_order, second_order),
        shape((parts, square + tiles * slots, LANES), BF16),
        [wide, total, gated, narrow, entries, entries, *parted],
        (),
        (bias_all, normed, pair_near, known_start, *near),
    )
    columns = exchange(sent, second_order)
    gain_near, shift_near, _, *near = near
    ended = call(
        functools.partial(end_kernel, second_order),
        shape((n * rows, C), BF16),
        [wide, total, gated, entries, *parted],
        (),
        (columns, known_end, gain_near, shift_near, *near),
    )
    return ended.reshape(n, rows, C)


def solution(mesh):
    in_specs = (
        P(("grp", "row", "sub"), None, None),
        P("grp"),
        P("grp"),
        P(),
        P(),
        P(),
        P(),
        P(),
        P(),
        P(),
        P(),
    )
    out_specs = P("grp", ("row", "sub"), None)
    return jax.shard_map(local, mesh=mesh, in_specs=in_specs, out_specs=out_specs, check_vma=False)
```

```python
import functools

import jax
import jax.numpy as jnp
from jax import lax
from jax.experimental import pallas as pl
from jax.experimental.pallas import tpu as pltpu
from jax.sharding import PartitionSpec as P

C = 128
HEADS = 4
HEAD_DIM = 32
HD = 128
LANES = 128
EPS = 1e-05

F32 = jnp.float32
BF16 = jnp.bfloat16
NN = (((1,), (0,)), ((), ()))
NT = (((1,), (1,)), ((), ()))


def matmul(a, b, dims=NN):
    return lax.dot_general(a, b, dims, preferred_element_type=F32)


def layer_norm(values, gain_row, shift_row):
    middle = jnp.mean(values, axis=-1, keepdims=True)
    centred = values - middle
    spread = jnp.mean(jnp.square(centred), axis=-1, keepdims=True)
    return (centred * lax.rsqrt(spread + EPS) * gain_row + shift_row).astype(BF16)


def head_mask(head):
    lane = lax.broadcasted_iota(jnp.int32, (1, HD), 1)
    return jnp.where(lane // HEAD_DIM == head, 1.0, 0.0).astype(BF16)


def each(count, unrolled, body):
    if unrolled:
        for index in range(count):
            body(index)
    else:
        lax.fori_loop(0, count, lambda index, _: (body(index), 0)[1], 0)


def block(index, size):
    if isinstance(index, int):
        return slice(index * size, (index + 1) * size)
    return pl.ds(pl.multiple_of(index * size, size), size)


def column_of(row):
    n = row.shape[1]
    first = lax.broadcasted_iota(jnp.int32, (n, n), 0)
    second = lax.broadcasted_iota(jnp.int32, (n, n), 1)
    return jnp.sum(jnp.where(first == second, row, 0.0), axis=1, keepdims=True)


def known_logits(layer, mask, chain, chain_offset, total):
    n = total.shape[1]
    chain_row = chain[...].astype(F32)
    key_row = jnp.where(mask[...] > 0, 0.0, -1000000000.0).astype(F32)
    cross = column_of(chain_row) != chain_row
    for head in range(HEADS):
        total[block(head, n), :] = jnp.where(cross, chain_offset[layer, head], 0.0) + key_row


def add_bias(flip, order, received, first_slot, wide, known, total):
    n = total.shape[1]
    slots = wide.shape[0] // received.shape[0]
    for tile in range(n // LANES):
        first = first_slot + tile * slots
        for place, part in enumerate(order):
            wide[block(part, slots), :] = received[place, first : first + slots, :].astype(F32)
        span = block(tile, LANES)
        for head in range(HEADS):
            gathered = wide[pl.ds(head, n, stride=HEADS), :]
            if flip:
                here = block(head * (n // LANES) + tile, LANES)
                total[here, :] = gathered.T + known[here, :]
            else:
                here = block(head, n)
                total[here, span] = gathered + known[here, span]


def project(normed, weights, gate_row, queries, keys, values, gates, n):
    count = normed.shape[0] // n
    projected = matmul(normed, weights)
    scaled = (projected[:, :HD] * (HEAD_DIM ** (-0.5))).astype(BF16)
    keys[...] = projected[:, HD : 2 * HD].astype(BF16)
    held = projected[:, 2 * HD : 3 * HD].astype(BF16)
    gates[...] = jax.nn.sigmoid(projected[:, 3 * HD :].astype(BF16).astype(F32) + gate_row)
    for head in range(HEADS):
        own = head_mask(head)
        own_queries, own_values = scaled * own, held * own
        for row in range(count):
            queries[block(row * HEADS + head, n), :] = own_queries[block(row, n), :]
            values[block(row * HEADS + head, n), :] = own_values[block(row, n), :]


def attend(queries, keys, values, gates, total):
    n = keys.shape[0]
    logits = matmul(queries[...], keys[...], NT) + total[...]
    expon = jnp.exp(logits - jnp.max(logits, axis=-1, keepdims=True))
    weights = (expon / jnp.sum(expon, axis=-1, keepdims=True)).astype(BF16)
    beside = jnp.concatenate([weights[block(head, n), :] for head in range(HEADS)], axis=1)
    summed = matmul(beside, values[...])
    return (summed * gates[...]).astype(BF16)


def attend_all(queries, keys, values, gates, total, gated):
    n = total.shape[1]

    def step(index):
        here, broad = block(index, n), block(index, HEADS * n)
        gated[here, :] = attend(
            queries.at[broad, :], keys.at[here, :], values.at[broad, :], gates.at[here, :], total
        )

    each(keys.shape[0] // n, n <= LANES, step)


def bias_rows(entries, layer, ln_gain, ln_shift, w_bias, narrow):
    normed = layer_norm(
        entries, ln_gain[layer : layer + 1, :], ln_shift[layer : layer + 1, :]
    )
    bias = matmul(w_bias[layer], normed, NT)
    n = narrow.shape[1]
    for row in range(entries.shape[0] // n):
        narrow[block(row, HEADS), :] = bias[:, block(row, n)]
    return normed


def pack_bias(narrow, first_slot, out):
    parts, (slots, n) = out.shape[0], narrow.shape
    for tile in range(n // LANES):
        part = narrow[:, block(tile, LANES)].astype(BF16)
        first = first_slot + tile * slots
        out[:, first : first + slots, :] = jnp.broadcast_to(part[None], (parts, slots, LANES))


def fetch(pairs, sems):
    copies = [
        pltpu.make_async_copy(far, near, sems.at[index]) for index, (far, near) in enumerate(pairs)
    ]
    for copy in copies:
        copy.start()
    return copies


def bias_kernel(
    pair_far, mask_far, chain_far, offset_far, gain_far, shift_far, bias_far, gate_far, out_far,
    w_qkvg_far, w_out_far,
    out, normed, known_start, known_end, pair, ln_gain, ln_shift, w_bias, gate_bias, out_bias, w_qkvg, w_out,
    mask, chain, chain_offset, narrow, sems,
):
    moves = (
        (pair_far, pair), (mask_far, mask), (chain_far, chain), (offset_far, chain_offset),
        (gain_far, ln_gain), (shift_far, ln_shift), (bias_far, w_bias), (gate_far, gate_bias),
        (out_far, out_bias), (w_qkvg_far, w_qkvg), (w_out_far, w_out),
    )
    copies = [
        pltpu.make_async_copy(far, near, sems.at[index]) for index, (far, near) in enumerate(moves)
    ]
    for copy in copies:
        copy.start()
    for copy in copies[1:7]:
        copy.wait()
    known_logits(0, mask, chain, chain_offset, known_start)
    known_logits(1, mask, chain, chain_offset, known_end)
    copies[0].wait()
    normed[...] = bias_rows(pair[...].astype(F32), 0, ln_gain, ln_shift, w_bias, narrow)
    pack_bias(narrow, 0, out)
    for copy in copies[7:]:
        copy.wait()


def start_kernel(
    first_order, second_order, received, normed, pair, known, ln_gain, ln_shift, w_bias, gate_bias,
    out_bias, w_qkvg, w_out, out, wide, total, gated, narrow, column, packed, queries, keys, values, gates,
):
    parts, n = out.shape[0], total.shape[1]
    rows = pair.shape[0] // n
    square = rows * rows

    add_bias(False, first_order, received, 0, wide, known, total)
    project(normed[...], w_qkvg[0], gate_bias[0:1, :], queries, keys, values, gates, n)
    attend_all(queries, keys, values, gates, total, gated)
    update = matmul(gated[...], w_out[0]) + out_bias[0:1, :]
    started = (pair[...].astype(F32) + update).astype(BF16).astype(F32)
    column[...] = started
    bias_rows(started, 1, ln_gain, ln_shift, w_bias, narrow)
    for row in range(rows):
        for place in range(rows):
            packed[pl.ds(row * rows + place, parts, stride=square), :] = column[
                pl.ds(row * n + place, parts, stride=rows), :
            ]
    for place, part in enumerate(second_order):
        out[place, :square, :] = packed[block(part, square), :].astype(BF16)
    pack_bias(narrow, square, out)


def end_kernel(
    order, received, known, ln_gain, ln_shift, gate_bias, out_bias, w_qkvg, w_out, out, wide, total, gated,
    packed, queries, keys, values, gates,
):
    n = total.shape[1]
    rows = packed.shape[0] // n
    square = rows * rows
    for place, part in enumerate(order):
        packed[block(part, square), :] = received[place, :square, :].astype(F32)

    add_bias(True, order, received, square, wide, known, total)
    entries = jnp.concatenate([packed[pl.ds(place, n, stride=rows), :] for place in range(rows)], axis=0)
    normed = layer_norm(entries, ln_gain[1:2, :], ln_shift[1:2, :])
    project(normed, w_qkvg[1], gate_bias[1:2, :], queries, keys, values, gates, n)
    attend_all(queries, keys, values, gates, total, gated)
    update = matmul(gated[...], w_out[1]) + out_bias[1:2, :]
    for place in range(rows):
        stripe = pl.ds(place, n, stride=rows)
        packed[stripe, :] = packed[stripe, :] + update[block(place, n), :]
    out[...] = packed[...].astype(BF16)


NEAR = pl.BlockSpec(memory_space=pltpu.VMEM)
FAR = pl.BlockSpec(memory_space=pltpu.HBM)


def call(kernel, out_shape, scratch, far, near):
    far = [pltpu.with_memory_space_constraint(array, pltpu.HBM) for array in far]
    return pl.pallas_call(
        kernel,
        out_shape=out_shape,
        in_specs=[FAR] * len(far) + [NEAR] * len(near),
        out_specs=jax.tree.map(lambda _: NEAR, out_shape),
        scratch_shapes=scratch,
        compiler_params=pltpu.CompilerParams(vmem_limit_bytes=40 * 1024 * 1024),
    )(*far, *near)


def exchange(array, order):
    return lax.all_to_all(
        array, ("row", "sub"), split_axis=0, concat_axis=0, tiled=True, axis_index_groups=[order]
    )


def orders(outer, inner):
    natural = list(range(outer * inner))
    pair = 2 if outer % 2 == 0 else 1
    apart = [
        (place * pair + half) * inner + part
        for half in range(pair)
        for part in range(inner)
        for place in range(outer // pair)
    ]
    return natural[::-1], apart[::-1]


def local(
    pair, mask, chain, ln_gain, ln_shift, w_qkvg, gate_bias, w_bias, w_out, out_bias, chain_offset
):
    rows, n = pair.shape[0], pair.shape[1]
    parts = lax.axis_size("row") * lax.axis_size("sub")
    tiles, slots, square = n // LANES, rows * HEADS, rows * rows
    first_order, second_order = orders(lax.axis_size("row"), lax.axis_size("sub"))
    shape = jax.ShapeDtypeStruct

    def like(*arrays):
        return [shape(array.shape, array.dtype) for array in arrays]

    flat = pair.reshape(rows * n, C)
    mask_row, chain_row = mask.reshape(1, n), chain.reshape(1, n)
    wide = pltpu.VMEM((parts * slots, LANES), F32)
    total = pltpu.VMEM((HEADS * n, n), F32)
    narrow = pltpu.VMEM((slots, n), F32)
    gated = pltpu.VMEM((rows * n, HD), BF16)
    entries = pltpu.VMEM((rows * n, C), F32)
    parted = [
        pltpu.VMEM((rows * HEADS * n, HD), BF16),
        pltpu.VMEM((rows * n, HD), BF16),
        pltpu.VMEM((rows * HEADS * n, HD), BF16),
        pltpu.VMEM((rows * n, HD), F32),
    ]
    known = shape((HEADS * n, n), F32)
    kept = (ln_gain, ln_shift, w_bias, gate_bias, out_bias, w_qkvg, w_out)
    bias_part, normed, known_start, known_end, pair_near, *near = call(
        bias_kernel,
        [shape((parts, tiles * slots, LANES), BF16), shape((rows * n, C), BF16), known, known]
        + like(flat, *kept),
        [
            pltpu.VMEM((1, n), jnp.int32),
            pltpu.VMEM((1, n), jnp.int32),
            pltpu.SMEM(chain_offset.shape, F32),
            narrow,
            pltpu.SemaphoreType.DMA((11,)),
        ],
        (flat, mask_row, chain_row, chain_offset, *kept),
        (),
    )
    bias_all = exchange(bias_part, first_order)
    sent = call(
        functools.partial(start_kernel, first_order, second_order),
        shape((parts, square + tiles * slots, LANES), BF16),
        [wide, total, gated, narrow, entries, entries, *parted],
        (),
        (bias_all, normed, pair_near, known_start, *near),
    )
    columns = exchange(sent, second_order)
    gain_near, shift_near, _, *near = near
    ended = call(
        functools.partial(end_kernel, second_order),
        shape((n * rows, C), BF16),
        [wide, total, gated, entries, *parted],
        (),
        (columns, known_end, gain_near, shift_near, *near),
    )
    return ended.reshape(n, rows, C)


def solution(mesh):
    in_specs = (
        P(("grp", "row", "sub"), None, None),
        P("grp"),
        P("grp"),
        P(),
        P(),
        P(),
        P(),
        P(),
        P(),
        P(),
        P(),
    )
    out_specs = P("grp", ("row", "sub"), None)
    return jax.shard_map(local, mesh=mesh, in_specs=in_specs, out_specs=out_specs, check_vma=False)
```

```python
import functools

import jax
import jax.numpy as jnp
from jax import lax
from jax.experimental import pallas as pl
from jax.experimental.pallas import tpu as pltpu
from jax.sharding import PartitionSpec as P

C = 128
HEADS = 4
HEAD_DIM = 32
HD = 128
LANES = 128
EPS = 1e-05

F32 = jnp.float32
BF16 = jnp.bfloat16
NN = (((1,), (0,)), ((), ()))
NT = (((1,), (1,)), ((), ()))


def matmul(a, b, dims=NN):
    return lax.dot_general(a, b, dims, preferred_element_type=F32)


def layer_norm(values, gain_row, shift_row):
    middle = jnp.mean(values, axis=-1, keepdims=True)
    centred = values - middle
    spread = jnp.mean(jnp.square(centred), axis=-1, keepdims=True)
    return (centred * lax.rsqrt(spread + EPS) * gain_row + shift_row).astype(BF16)


def head_mask(head):
    lane = lax.broadcasted_iota(jnp.int32, (1, HD), 1)
    return jnp.where(lane // HEAD_DIM == head, 1.0, 0.0).astype(BF16)


def each(count, unrolled, body):
    if unrolled:
        for index in range(count):
            body(index)
    else:
        lax.fori_loop(0, count, lambda index, _: (body(index), 0)[1], 0)


def block(index, size):
    if isinstance(index, int):
        return slice(index * size, (index + 1) * size)
    return pl.ds(pl.multiple_of(index * size, size), size)


def column_of(row):
    n = row.shape[1]
    first = lax.broadcasted_iota(jnp.int32, (n, n), 0)
    second = lax.broadcasted_iota(jnp.int32, (n, n), 1)
    return jnp.sum(jnp.where(first == second, row, 0.0), axis=1, keepdims=True)


def known_logits(layer, mask, chain, chain_offset, total):
    n = total.shape[1]
    chain_row = chain[...].astype(F32)
    key_row = jnp.where(mask[...] > 0, 0.0, -1000000000.0).astype(F32)
    cross = column_of(chain_row) != chain_row
    for head in range(HEADS):
        total[block(head, n), :] = jnp.where(cross, chain_offset[layer, head], 0.0) + key_row


def add_bias(flip, order, received, first_slot, wide, known, total):
    n = total.shape[1]
    slots = wide.shape[0] // received.shape[0]
    for tile in range(n // LANES):
        first = first_slot + tile * slots
        for place, part in enumerate(order):
            wide[block(part, slots), :] = received[place, first : first + slots, :].astype(F32)
        span = block(tile, LANES)
        for head in range(HEADS):
            gathered = wide[pl.ds(head, n, stride=HEADS), :]
            if flip:
                here = block(head * (n // LANES) + tile, LANES)
                total[here, :] = gathered.T + known[here, :]
            else:
                here = block(head, n)
                total[here, span] = gathered + known[here, span]


def project(normed, weights, gate_row, queries, keys, values, gates, n):
    count = normed.shape[0] // n
    projected = matmul(normed, weights)
    scaled = (projected[:, :HD] * (HEAD_DIM ** (-0.5))).astype(BF16)
    keys[...] = projected[:, HD : 2 * HD].astype(BF16)
    held = projected[:, 2 * HD : 3 * HD].astype(BF16)
    gate_logits = projected[:, 3 * HD :].astype(BF16).astype(F32) + gate_row
    gates[...] = 0.5 * jnp.tanh(0.5 * gate_logits) + 0.5
    for head in range(HEADS):
        own = head_mask(head)
        own_queries, own_values = scaled * own, held * own
        for row in range(count):
            queries[block(row * HEADS + head, n), :] = own_queries[block(row, n), :]
            values[block(row * HEADS + head, n), :] = own_values[block(row, n), :]


def attend(queries, keys, values, gates, total):
    n = keys.shape[0]
    logits = matmul(queries[...], keys[...], NT) + total[...]
    expon = jnp.exp(logits - jnp.max(logits, axis=-1, keepdims=True))
    weights = (expon / jnp.sum(expon, axis=-1, keepdims=True)).astype(BF16)
    beside = jnp.concatenate([weights[block(head, n), :] for head in range(HEADS)], axis=1)
    summed = matmul(beside, values[...])
    return (summed * gates[...]).astype(BF16)


def attend_all(queries, keys, values, gates, total, gated):
    n = total.shape[1]

    def step(index):
        here, broad = block(index, n), block(index, HEADS * n)
        gated[here, :] = attend(
            queries.at[broad, :], keys.at[here, :], values.at[broad, :], gates.at[here, :], total
        )

    each(keys.shape[0] // n, n <= LANES, step)


def bias_rows(entries, layer, ln_gain, ln_shift, w_bias, narrow):
    normed = layer_norm(
        entries, ln_gain[layer : layer + 1, :], ln_shift[layer : layer + 1, :]
    )
    bias = matmul(w_bias[layer], normed, NT)
    n = narrow.shape[1]
    for row in range(entries.shape[0] // n):
        narrow[block(row, HEADS), :] = bias[:, block(row, n)]
    return normed


def pack_bias(narrow, first_slot, out):
    parts, (slots, n) = out.shape[0], narrow.shape
    for tile in range(n // LANES):
        part = narrow[:, block(tile, LANES)].astype(BF16)
        first = first_slot + tile * slots
        out[:, first : first + slots, :] = jnp.broadcast_to(part[None], (parts, slots, LANES))


def fetch(pairs, sems):
    copies = [
        pltpu.make_async_copy(far, near, sems.at[index]) for index, (far, near) in enumerate(pairs)
    ]
    for copy in copies:
        copy.start()
    return copies


def bias_kernel(
    pair_far, mask_far, chain_far, offset_far, gain_far, shift_far, bias_far, gate_far, out_far,
    w_qkvg_far, w_out_far,
    out, normed, known_start, known_end, pair, ln_gain, ln_shift, w_bias, gate_bias, out_bias, w_qkvg, w_out,
    mask, chain, chain_offset, narrow, sems,
):
    moves = (
        (pair_far, pair), (mask_far, mask), (chain_far, chain), (offset_far, chain_offset),
        (gain_far, ln_gain), (shift_far, ln_shift), (bias_far, w_bias), (gate_far, gate_bias),
        (out_far, out_bias), (w_qkvg_far, w_qkvg), (w_out_far, w_out),
    )
    copies = [
        pltpu.make_async_copy(far, near, sems.at[index]) for index, (far, near) in enumerate(moves)
    ]
    for copy in copies:
        copy.start()
    for copy in copies[:7]:
        copy.wait()
    normed[...] = bias_rows(pair[...].astype(F32), 0, ln_gain, ln_shift, w_bias, narrow)
    pack_bias(narrow, 0, out)
    known_logits(0, mask, chain, chain_offset, known_start)
    known_logits(1, mask, chain, chain_offset, known_end)
    for copy in copies[7:]:
        copy.wait()


def start_kernel(
    first_order, second_order, received, normed, pair, known, ln_gain, ln_shift, w_bias, gate_bias,
    out_bias, w_qkvg, w_out, out, wide, total, gated, narrow, column, packed, queries, keys, values, gates,
):
    parts, n = out.shape[0], total.shape[1]
    rows = pair.shape[0] // n
    square = rows * rows

    add_bias(False, first_order, received, 0, wide, known, total)
    project(normed[...], w_qkvg[0], gate_bias[0:1, :], queries, keys, values, gates, n)
    attend_all(queries, keys, values, gates, total, gated)
    update = matmul(gated[...], w_out[0]) + out_bias[0:1, :]
    started = (pair[...].astype(F32) + update).astype(BF16).astype(F32)
    column[...] = started
    bias_rows(started, 1, ln_gain, ln_shift, w_bias, narrow)
    for row in range(rows):
        for place in range(rows):
            packed[pl.ds(row * rows + place, parts, stride=square), :] = column[
                pl.ds(row * n + place, parts, stride=rows), :
            ]
    for place, part in enumerate(second_order):
        out[place, :square, :] = packed[block(part, square), :].astype(BF16)
    pack_bias(narrow, square, out)


def end_kernel(
    order, received, known, ln_gain, ln_shift, gate_bias, out_bias, w_qkvg, w_out, out, wide, total, gated,
    packed, queries, keys, values, gates,
):
    n = total.shape[1]
    rows = packed.shape[0] // n
    square = rows * rows
    for place, part in enumerate(order):
        packed[block(part, square), :] = received[place, :square, :].astype(F32)

    add_bias(True, order, received, square, wide, known, total)
    entries = jnp.concatenate([packed[pl.ds(place, n, stride=rows), :] for place in range(rows)], axis=0)
    normed = layer_norm(entries, ln_gain[1:2, :], ln_shift[1:2, :])
    project(normed, w_qkvg[1], gate_bias[1:2, :], queries, keys, values, gates, n)
    attend_all(queries, keys, values, gates, total, gated)
    update = matmul(gated[...], w_out[1]) + out_bias[1:2, :]
    for place in range(rows):
        stripe = pl.ds(place, n, stride=rows)
        packed[stripe, :] = entries[block(place, n), :] + update[block(place, n), :]
    out[...] = packed[...].astype(BF16)


NEAR = pl.BlockSpec(memory_space=pltpu.VMEM)
FAR = pl.BlockSpec(memory_space=pltpu.HBM)


def call(kernel, out_shape, scratch, far, near):
    far = [pltpu.with_memory_space_constraint(array, pltpu.HBM) for array in far]
    return pl.pallas_call(
        kernel,
        out_shape=out_shape,
        in_specs=[FAR] * len(far) + [NEAR] * len(near),
        out_specs=jax.tree.map(lambda _: NEAR, out_shape),
        scratch_shapes=scratch,
        compiler_params=pltpu.CompilerParams(vmem_limit_bytes=40 * 1024 * 1024),
    )(*far, *near)


def exchange(array, order):
    return lax.all_to_all(
        array, ("row", "sub"), split_axis=0, concat_axis=0, tiled=True, axis_index_groups=[order]
    )


def orders(outer, inner):
    natural = list(range(outer * inner))
    pair = 2 if outer % 2 == 0 else 1
    apart = [
        (place * pair + half) * inner + part
        for half in range(pair)
        for part in range(inner)
        for place in range(outer // pair)
    ]
    return natural[::-1], apart[::-1]


def local(
    pair, mask, chain, ln_gain, ln_shift, w_qkvg, gate_bias, w_bias, w_out, out_bias, chain_offset
):
    rows, n = pair.shape[0], pair.shape[1]
    parts = lax.axis_size("row") * lax.axis_size("sub")
    tiles, slots, square = n // LANES, rows * HEADS, rows * rows
    first_order, second_order = orders(lax.axis_size("row"), lax.axis_size("sub"))
    shape = jax.ShapeDtypeStruct

    def like(*arrays):
        return [shape(array.shape, array.dtype) for array in arrays]

    flat = pair.reshape(rows * n, C)
    mask_row, chain_row = mask.reshape(1, n), chain.reshape(1, n)
    wide = pltpu.VMEM((parts * slots, LANES), F32)
    total = pltpu.VMEM((HEADS * n, n), F32)
    narrow = pltpu.VMEM((slots, n), F32)
    gated = pltpu.VMEM((rows * n, HD), BF16)
    entries = pltpu.VMEM((rows * n, C), F32)
    parted = [
        pltpu.VMEM((rows * HEADS * n, HD), BF16),
        pltpu.VMEM((rows * n, HD), BF16),
        pltpu.VMEM((rows * HEADS * n, HD), BF16),
        pltpu.VMEM((rows * n, HD), F32),
    ]
    known = shape((HEADS * n, n), F32)
    kept = (ln_gain, ln_shift, w_bias, gate_bias, out_bias, w_qkvg, w_out)
    bias_part, normed, known_start, known_end, pair_near, *near = call(
        bias_kernel,
        [shape((parts, tiles * slots, LANES), BF16), shape((rows * n, C), BF16), known, known]
        + like(flat, *kept),
        [
            pltpu.VMEM((1, n), jnp.int32),
            pltpu.VMEM((1, n), jnp.int32),
            pltpu.SMEM(chain_offset.shape, F32),
            narrow,
            pltpu.SemaphoreType.DMA((11,)),
        ],
        (flat, mask_row, chain_row, chain_offset, *kept),
        (),
    )
    bias_all = exchange(bias_part, first_order)
    sent = call(
        functools.partial(start_kernel, first_order, second_order),
        shape((parts, square + tiles * slots, LANES), BF16),
        [wide, total, gated, narrow, entries, entries, *parted],
        (),
        (bias_all, normed, pair_near, known_start, *near),
    )
    columns = exchange(sent, second_order)
    gain_near, shift_near, _, *near = near
    ended = call(
        functools.partial(end_kernel, second_order),
        shape((n * rows, C), BF16),
        [wide, total, gated, entries, *parted],
        (),
        (columns, known_end, gain_near, shift_near, *near),
    )
    return ended.reshape(n, rows, C)


def solution(mesh):
    in_specs = (
        P(("grp", "row", "sub"), None, None),
        P("grp"),
        P("grp"),
        P(),
        P(),
        P(),
        P(),
        P(),
        P(),
        P(),
        P(),
    )
    out_specs = P("grp", ("row", "sub"), None)
    return jax.shard_map(local, mesh=mesh, in_specs=in_specs, out_specs=out_specs, check_vma=False)
```
